256 devices in a mesh: dp: 8 (over y, z_hi), tensor: 32 (over z_lo, x, core).
Axes of the slice: x: 4, y: 4, z: 8 (z_hi: 2, z_lo: 4; z = z_hi * 4 + z_lo), core: 2. Of those that a mesh axis runs over, the one named last changes fastest.
Arguments:
- inputs: float32 [1024, 4096], P('dp', 'tensor'), may hold values from -6 to 6
- out_grad: float32 [1024, 4096], P('dp', 'tensor'), may hold values from -6 to 6
- up_weight: float32 [768, 128, 128], P('tensor'), may hold values from -0.25 to 0.25
- down_weight: float32 [768, 128, 128], P('tensor'), may hold values from -0.109375 to 0.109375
- up_left: float32 [4096, 128], P('tensor'), may hold values from -0.09375 to 0.09375
- up_right: float32 [128, 16384], P(None, 'tensor'), may hold values from -0.5 to 0.5
- down_left: float32 [16384, 128], P('tensor'), may hold values from -0.046875 to 0.046875
- down_right: float32 [128, 4096], P(None, 'tensor'), may hold values from -0.5 to 0.5
- model_block: int32 [768], P('tensor'), may hold values from 0 to 31, as said below
- hidden_block: int32 [768], P('tensor'), may hold values from 0 to 3
- live_slots: int32 [32], P('tensor'), may hold values from 12 to 24, as said below
Outputs:
- result: float32 [1024, 4096], P('dp', 'tensor')
- input_grad: float32 [1024, 4096], P('dp', 'tensor')
- up_grad: float32 [768, 128, 128], P('tensor', 'dp')
- down_grad: float32 [768, 128, 128], P('tensor', 'dp')
- up_left_grad: float32 [4096, 128], P(('tensor', 'dp'))
- up_right_grad: float32 [128, 16384], P('dp', 'tensor')
- down_left_grad: float32 [16384, 128], P(('tensor', 'dp'))
- down_right_grad: float32 [128, 4096], P('dp', 'tensor')
The draws below stay inside these ranges and needn't reach their ends.
Inputs may be any that keep to these rules, and one draw needn't show every extreme that they name: `model_block`: with g the slot's hidden block counted over all owners, the slot's model block differs from g mod 32 in at most one bit. `live_slots`: at least one owner has all 24 slots live.
All inputs are finite; a program needn't handle non-finite values.
Results may differ from the reference program's by a relative error of at most 0.0003.
Values sent between devices are 32-bit elements; how exact they have to be, the bound alone decides.
No kernel may reach another device: no remote copies, remote signals or barrier semaphores. Data moves between devices by JAX's collectives and lax.ppermute only.
A program may use at most 64 MiB of HBM per device.

```python
import jax
import jax.numpy as jnp
from jax import lax

D = 4096
FF = 16384
BLK = 128
RANK = 128
TOKENS = 1024
DBLOCKS = 32
HBLOCKS = 4
CAP = 24
OWNERS = 32
SLOTS = 768


def slot_pattern(key):
    folded = jax.random.fold_in(key, 7)
    key_hidden, key_level = jax.random.split(folded)
    hidden = jax.random.randint(key_hidden, (SLOTS,), 0, HBLOCKS, dtype=jnp.int32)
    levels = DBLOCKS.bit_length() - 1
    section_bit = jax.random.randint(key_level, (SLOTS,), 0, levels + 1, dtype=jnp.int32)
    owner_id = jnp.arange(SLOTS, dtype=jnp.int32) // CAP
    column = (owner_id * HBLOCKS + hidden) % DBLOCKS
    toggled = jnp.where(section_bit == levels, jnp.int32(0), jnp.left_shift(jnp.int32(1), jnp.minimum(section_bit, levels - 1)))
    return (hidden, jnp.bitwise_xor(column, toggled))


def draw_model_block(key, part):
    return slot_pattern(key)[1]


def draw_hidden_block(key, part):
    return slot_pattern(key)[0]


def draw_live_slots(key, part):
    folded = jax.random.fold_in(key, 13)
    key_count, key_full = jax.random.split(folded)
    counted = jax.random.randint(key_count, (OWNERS,), CAP // 2, CAP + 1, dtype=jnp.int32)
    full_owner = jax.random.randint(key_full, (), 0, OWNERS, dtype=jnp.int32)
    return jnp.where(jnp.arange(OWNERS, dtype=jnp.int32) == full_owner, jnp.int32(CAP), counted)


def level_of(stream_key, shape, cuts, least, top_value):
    def one(axis_at, blocks):
        draws = jax.random.uniform(jax.random.fold_in(jax.random.fold_in(stream_key, 6), axis_at), (blocks,), jnp.float32, least / len(cuts), top_value / len(cuts))
        return jnp.repeat(jnp.exp(draws), shape[axis_at] // blocks).reshape((-1,) + (1,) * (len(shape) - axis_at - 1))

    level = one(*cuts[0])
    for cut in cuts[1:]:
        level = level * one(*cut)
    return level


def gaussian(rng, shape, width, reach, cuts=(), kind=jnp.bfloat16):
    loudness = level_of(rng, shape, cuts, -0.22, 0.18) if cuts else 1.0
    array = jax.random.normal(rng, shape, jnp.float32) * width * loudness
    return jnp.minimum(jnp.maximum(array, -reach), reach).astype(kind)


def setup_inputs(seed: int = 0) -> dict:
    key_of = jax.random.split(jax.random.key(seed), 12)
    return {
        "inputs": gaussian(key_of[0], (TOKENS, D), 1.0, 6.0, ((0, 8), (1, 32)), jnp.float32),
        "out_grad": gaussian(key_of[1], (TOKENS, D), 1.0, 6.0, ((0, 8), (1, 32)), jnp.float32),
        "up_weight": gaussian(key_of[2], (SLOTS, BLK, BLK), (5 * BLK) ** -0.5, 0.25, ((0, 32),), jnp.float32),
        "down_weight": gaussian(key_of[3], (SLOTS, BLK, BLK), (SLOTS * BLK // DBLOCKS) ** -0.5, 0.109375, ((0, 32),), jnp.float32),
        "up_left": gaussian(key_of[4], (D, RANK), D ** -0.5, 0.09375, ((0, 32),), jnp.float32),
        "up_right": gaussian(key_of[5], (RANK, FF), RANK ** -0.5, 0.5, ((1, 32),), jnp.float32),
        "down_left": gaussian(key_of[6], (FF, RANK), FF ** -0.5, 0.046875, ((0, 32),), jnp.float32),
        "down_right": gaussian(key_of[7], (RANK, D), RANK ** -0.5, 0.5, ((1, 32),), jnp.float32),
        "model_block": draw_model_block(jax.random.fold_in(key_of[11], 71), 0),
        "hidden_block": draw_hidden_block(jax.random.fold_in(key_of[11], 71), 0),
        "live_slots": draw_live_slots(jax.random.fold_in(key_of[11], 71), 0),
    }


highest = lax.Precision.HIGHEST

def activation(values):
    return jax.nn.gelu(values, approximate=True)

def onehot(indices, extent):
    return (indices[:, None] == jnp.arange(extent, dtype=jnp.int32)[None, :]).astype(jnp.float32)

def reference(inputs, out_grad, up_weight, down_weight, up_left, up_right, down_left, down_right, model_block, hidden_block, live_slots):
    row_count = inputs.shape[0]
    hidden_width = HBLOCKS * BLK
    slot_index = jnp.arange(SLOTS, dtype=jnp.int32)
    owner_id = slot_index // CAP
    alive_mask = (slot_index % CAP < live_slots[owner_id]).astype(jnp.float32)
    up_live = (up_weight * alive_mask[:, None, None]).reshape(OWNERS, CAP, BLK, BLK)
    down_live = (down_weight * alive_mask[:, None, None]).reshape(OWNERS, CAP, BLK, BLK)
    model_owned = model_block.reshape(OWNERS, CAP)
    hidden_owned = hidden_block.reshape(OWNERS, CAP)
    alive_owned = alive_mask.reshape(OWNERS, CAP)
    right_owned = up_right.reshape(RANK, OWNERS, hidden_width).transpose(1, 0, 2)
    left_owned = down_left.reshape(OWNERS, hidden_width, RANK)
    split_in = inputs.reshape(row_count, DBLOCKS, BLK)
    split_grad = out_grad.reshape(row_count, DBLOCKS, BLK)
    low_in = jnp.dot(inputs, up_left, precision=highest)

    def forward_up(running, pieces):
        weight, models, hiddens, right = pieces
        chosen = jnp.take(split_in, models, axis=1)
        slot_out = jnp.einsum('tsk,skn->tsn', chosen, weight, precision=highest)
        merged = jnp.einsum('tsn,sh->thn', slot_out, onehot(hiddens, HBLOCKS), precision=highest)
        return (running, merged.reshape(row_count, hidden_width) + jnp.dot(low_in, right, precision=highest))
    _, preact = lax.scan(forward_up, jnp.zeros((), jnp.float32), (up_live, model_owned, hidden_owned, right_owned))
    hidden = activation(preact)
    low_mid = jnp.einsum('otw,owr->tr', hidden, left_owned, precision=highest)

    def forward_down(running, pieces):
        weight, models, hiddens, hidden_part = pieces
        chosen = jnp.take(hidden_part.reshape(row_count, HBLOCKS, BLK), hiddens, axis=1)
        slot_out = jnp.einsum('tsk,skn->tsn', chosen, weight, precision=highest)
        placed = jnp.einsum('tsn,sm->tmn', slot_out, onehot(models, DBLOCKS), precision=highest)
        return (running + placed.reshape(row_count, D), jnp.zeros((), jnp.float32))
    sparse_out, _ = lax.scan(forward_down, jnp.zeros((row_count, D), jnp.float32), (down_live, model_owned, hidden_owned, hidden))
    result = sparse_out + jnp.dot(low_mid, down_right, precision=highest)
    back_mid = jnp.dot(out_grad, down_right.T, precision=highest)

    def backward_down(running, pieces):
        weight, models, hiddens, alive, hidden_part, preact_part, left = pieces
        chosen_grad = jnp.take(split_grad, models, axis=1)
        slot_back = jnp.einsum('tsn,skn->tsk', chosen_grad, weight, precision=highest)
        merged = jnp.einsum('tsk,sh->thk', slot_back, onehot(hiddens, HBLOCKS), precision=highest)
        hidden_grad = merged.reshape(row_count, hidden_width) + jnp.dot(back_mid, left.T, precision=highest)
        _, pullback = jax.vjp(activation, preact_part)
        preact_grad = pullback(hidden_grad)[0]
        chosen_hidden = jnp.take(hidden_part.reshape(row_count, HBLOCKS, BLK), hiddens, axis=1)
        weight_grad = jnp.einsum('tsk,tsn->skn', chosen_hidden, chosen_grad, precision=highest) * alive[:, None, None]
        left_grad = jnp.dot(hidden_part.T, back_mid, precision=highest)
        return (running, (preact_grad, weight_grad, left_grad))
    _, (preact_grad, down_grad, down_left_grad) = lax.scan(backward_down, jnp.zeros((), jnp.float32), (down_live, model_owned, hidden_owned, alive_owned, hidden, preact, left_owned))
    back_in = jnp.einsum('otw,orw->tr', preact_grad, right_owned, precision=highest)

    def backward_up(running, pieces):
        weight, models, hiddens, alive, grad_part = pieces
        chosen_grad = jnp.take(grad_part.reshape(row_count, HBLOCKS, BLK), hiddens, axis=1)
        slot_back = jnp.einsum('tsn,skn->tsk', chosen_grad, weight, precision=highest)
        placed = jnp.einsum('tsk,sm->tmk', slot_back, onehot(models, DBLOCKS), precision=highest)
        chosen_in = jnp.take(split_in, models, axis=1)
        weight_grad = jnp.einsum('tsk,tsn->skn', chosen_in, chosen_grad, precision=highest) * alive[:, None, None]
        return (running + placed.reshape(row_count, D), weight_grad)
    sparse_in, up_grad = lax.scan(backward_up, jnp.zeros((row_count, D), jnp.float32), (up_live, model_owned, hidden_owned, alive_owned, preact_grad))
    input_grad = sparse_in + jnp.dot(back_in, up_left.T, precision=highest)
    up_left_grad = jnp.dot(inputs.T, back_in, precision=highest)
    up_right_grad = jnp.einsum('tr,otw->row', low_in, preact_grad, precision=highest).reshape(RANK, FF)
    down_right_grad = jnp.dot(low_mid.T, out_grad, precision=highest)
    return (result, input_grad, up_grad.reshape(SLOTS, BLK, BLK), down_grad.reshape(SLOTS, BLK, BLK), up_left_grad, up_right_grad, down_left_grad.reshape(FF, RANK), down_right_grad)
```

```python
import jax
import jax.numpy as jnp
from jax import lax
from jax.experimental import pallas as pl
from jax.experimental.pallas import tpu as pltpu
from jax.sharding import PartitionSpec as P

f32 = jnp.float32
highest = lax.Precision.HIGHEST
VMEM = pl.BlockSpec(memory_space=pltpu.VMEM)
SMEM = pl.BlockSpec(memory_space=pltpu.SMEM)
PARAMS = pltpu.CompilerParams(vmem_limit_bytes=48 * 1024 * 1024)
ROOT = 0.7978845608028654
CUBE = 0.044715
BATCH = 4

NN = ((1,), (0,))
NT = ((1,), (1,))
TN = ((0,), (0,))


def split(value):
    high = value.astype(jnp.bfloat16)
    return high, (value - high.astype(f32)).astype(jnp.bfloat16)


def dot3(left, right, dims):
    def one(a, b):
        return lax.dot_general(a, b, (dims, ((), ())), preferred_element_type=f32)

    return one(left[0], right[0]) + (one(left[0], right[1]) + one(left[1], right[0]))


def grads_kernel(
    model_ref, hidden_ref, live_ref, fields_ref, up_ref, down_ref, low_ref, right_ref, left_ref,
    total_ref, act_ref, pgrad_ref,
):
    rows = act_ref.shape[1]
    local_blocks = act_ref.shape[0]
    slot_count = up_ref.shape[0]
    parts = total_ref.shape[0]
    piece = total_ref.shape[2]
    live = live_ref[0]
    low_in = split(low_ref[0:rows])
    back_mid = split(low_ref[rows : 2 * rows])
    for h in range(local_blocks):
        span = slice(h * 128, (h + 1) * 128)
        act_ref[h] = dot3(low_in, split(right_ref[:, span]), NN)
        pgrad_ref[h] = dot3(back_mid, split(left_ref[span]), NT)

    @pl.loop(0, slot_count // BATCH)
    def _(step):
        terms = []
        for j in range(BATCH):
            s = step * BATCH + j
            m = model_ref[s]
            alive = jnp.where(s < live, 1.0, 0.0).astype(f32)
            up = dot3(split(fields_ref[m, 0:rows]), split(up_ref[s]), NN)
            back = dot3(split(fields_ref[m, rows : 2 * rows]), split(down_ref[s]), NT)
            terms.append((hidden_ref[s], up * alive, back * alive))
        for h, up, back in terms:
            act_ref[h] += up
            pgrad_ref[h] += back

    base = 2 * slot_count
    for h in range(local_blocks):
        value = act_ref[h]
        square = value * value
        bent = jnp.tanh(ROOT * (value + CUBE * (value * square)))
        half = 0.5 * (1.0 + bent)
        slope = half + 0.5 * value * (1.0 - bent * bent) * (ROOT * (1.0 + 3.0 * CUBE * square))
        hidden = value * half
        pgrad = pgrad_ref[h] * slope
        act_ref[h] = hidden
        pgrad_ref[h] = pgrad
        right_grad = dot3(low_in, split(pgrad), TN)
        total_ref[:, base + h] = right_grad.reshape(parts, piece, 128)
        left_grad = dot3(split(hidden), back_mid, TN)
        for t in range(parts):
            d, i = divmod(h * parts + t, local_blocks)
            total_ref[d, base + local_blocks + i] = left_grad[t * piece : (t + 1) * piece]

    @pl.loop(0, slot_count // BATCH)
    def _(step):
        for j in range(BATCH):
            s = step * BATCH + j
            m = model_ref[s]
            h = hidden_ref[s]
            alive = jnp.where(s < live, 1.0, 0.0).astype(f32)
            up = dot3(split(fields_ref[m, 0:rows]), split(pgrad_ref[h]), TN) * alive
            down = dot3(split(act_ref[h]), split(fields_ref[m, rows : 2 * rows]), TN) * alive
            total_ref[:, s] = up.reshape(parts, piece, 128)
            total_ref[:, slot_count + s] = down.reshape(parts, piece, 128)


def terms_kernel(
    place_ref, hidden_ref, live_ref, act_ref, pgrad_ref, up_ref, down_ref, right_ref, left_ref,
    keep_ref, send_ref, low_ref, sums,
):
    rows = act_ref.shape[1]
    local_blocks = act_ref.shape[0]
    slot_count = up_ref.shape[0]
    live = live_ref[0]
    low_mid = None
    back_in = None
    for h in range(local_blocks):
        span = slice(h * 128, (h + 1) * 128)
        mid = dot3(split(act_ref[h]), split(left_ref[span]), NN)
        back = dot3(split(pgrad_ref[h]), split(right_ref[:, span]), NT)
        low_mid = mid if low_mid is None else low_mid + mid
        back_in = back if back_in is None else back_in + back
    low_ref[0:rows] = low_mid
    low_ref[rows : 2 * rows] = back_in
    for p in range(2):
        for b in range(16):
            sums[p, b] = jnp.zeros((rows, 128), f32)

    @pl.loop(0, slot_count // BATCH)
    def _(step):
        terms = []
        for j in range(BATCH):
            s = step * BATCH + j
            h = hidden_ref[s]
            alive = jnp.where(s < live, 1.0, 0.0).astype(f32)
            out = dot3(split(act_ref[h]), split(down_ref[s]), NN) * alive
            back = dot3(split(pgrad_ref[h]), split(up_ref[s]), NT) * alive
            terms.append((place_ref[s], out, back))
        for b, out, back in terms:
            sums[0, b] += out
            sums[1, b] += back

    keep_ref[...] = sums[:, 0:8]
    send_ref[...] = sums[:, 8:16]


def xor_shift(value, bits):
    size = lax.axis_size("tensor")
    return lax.ppermute(value, "tensor", [(i, i ^ bits) for i in range(size)])


def exchange(value):
    return lax.all_to_all(value, "tensor", 0, 0, tiled=True)


def low_total(partial_value):
    size = lax.axis_size("tensor")
    pieces = exchange(partial_value.reshape(size, -1, 128)).sum(axis=0)
    spread = exchange(jnp.broadcast_to(pieces[None], (size,) + pieces.shape))
    return spread.reshape(partial_value.shape)


def block_total(keep, send, core, x, z):
    other = xor_shift(send, 1)
    first = (x // 2) ^ core
    mine = first == 0

    def merged(part):
        own, got = keep[part], other[part]
        zero = own[0:4] + got[0:4]
        rest = []
        for at in (4, 6):
            a, b = own[at : at + 2], got[at : at + 2]
            rest.append(jnp.concatenate([jnp.where(mine, a, b), jnp.where(mine, b, a)]))
        return jnp.stack([zero] + rest)

    def along_x(terms, near, far):
        mix = near ^ far
        got = xor_shift(jnp.stack([terms[:, near], terms[:, mix]]), near << 1)

        def value(f, pair, e):
            total = terms[f, e] if f < 3 else None
            if (f ^ near) < 3:
                add = got[pair, f ^ near]
                total = add if total is None else total + add
            return total

        more = xor_shift(jnp.stack([value(f, 1, far) for f in range(4)]), far << 1)
        return jnp.stack([value(f, 0, 0) + more[f ^ far] for f in range(4)])

    out = along_x(merged(0), 1, 3)
    back = along_x(merged(1), 3, 1)
    both = jnp.stack([out, back], axis=1)
    w = x ^ z
    pick = lambda at: lax.dynamic_index_in_dim(both, at, 0, keepdims=False)
    got = xor_shift(jnp.stack([pick(w ^ 1), pick(w ^ 3)]), 1 << 3)
    last = xor_shift(pick(w ^ 2) + got[1], 2 << 3)
    total = pick(w) + got[0] + last
    return total[0], total[1]


def shards(
    inputs, out_grad, up_weight, down_weight, up_left, up_right, down_left, down_right,
    model_block, hidden_block, live_slots,
):
    rows = inputs.shape[0]
    slot_count = up_weight.shape[0]
    local_blocks = up_right.shape[1] // 128
    parts = lax.axis_size("dp")
    piece = 128 // parts
    me = lax.axis_index("tensor").astype(jnp.int32)
    core, x, z = me & 1, (me >> 1) & 3, me >> 3
    e = ((model_block >> 1) & 3) ^ x
    zrel = (model_block >> 3) ^ x
    place = jnp.where(zrel == 0, e, 2 + 2 * zrel + (e & 1)) + 8 * ((model_block & 1) ^ core)

    fields = lax.all_gather(jnp.concatenate([inputs, out_grad]), "tensor")
    low = low_total(
        jnp.concatenate(
            [
                jnp.dot(inputs, up_left, precision=highest),
                lax.dot_general(out_grad, down_right, (NT, ((), ())), precision=highest),
            ]
        )
    )
    tiles = 2 * slot_count + 2 * local_blocks
    total, act, pgrad = pl.pallas_call(
        grads_kernel,
        out_shape=(
            jax.ShapeDtypeStruct((parts, tiles, piece, 128), f32),
            jax.ShapeDtypeStruct((local_blocks, rows, 128), f32),
            jax.ShapeDtypeStruct((local_blocks, rows, 128), f32),
        ),
        in_specs=[SMEM] * 3 + [VMEM] * 6,
        out_specs=(VMEM,) * 3,
        compiler_params=PARAMS,
        name="grads",
    )(model_block, hidden_block, live_slots, fields, up_weight, down_weight, low, up_right, down_left)
    shared = lax.psum_scatter(total, "dp", scatter_dimension=0, tiled=True)[0]
    keep, send, low_part = pl.pallas_call(
        terms_kernel,
        out_shape=(
            jax.ShapeDtypeStruct((2, 8, rows, 128), f32),
            jax.ShapeDtypeStruct((2, 8, rows, 128), f32),
            jax.ShapeDtypeStruct((2 * rows, 128), f32),
        ),
        in_specs=[SMEM] * 3 + [VMEM] * 6,
        out_specs=(VMEM,) * 3,
        scratch_shapes=[pltpu.VMEM((2, 16, rows, 128), f32)],
        compiler_params=PARAMS,
        name="terms",
    )(place, hidden_block, live_slots, act, pgrad, up_weight, down_weight, up_right, down_left)
    low_out = low_total(low_part)
    low_mid, back_in = low_out[:rows], low_out[rows:]
    left_part = lax.dot_general(inputs, back_in, (TN, ((), ())), precision=highest)
    right_part = lax.dot_general(low_mid, out_grad, (TN, ((), ())), precision=highest)
    ends = jnp.stack([left_part.reshape(parts, piece, 128), right_part.reshape(parts, piece, 128)], axis=1)
    ends = lax.all_to_all(ends, "dp", 0, 0, tiled=True).sum(axis=0)
    out, back = block_total(keep, send, core, x, z)
    result = out + jnp.dot(low_mid, down_right, precision=highest)
    input_grad = back + lax.dot_general(back_in, up_left, (NT, ((), ())), precision=highest)
    up_grad = shared[:slot_count]
    down_grad = shared[slot_count : 2 * slot_count]
    right_tiles = shared[2 * slot_count : 2 * slot_count + local_blocks]
    up_right_grad = right_tiles.transpose(1, 0, 2).reshape(piece, local_blocks * 128)
    down_left_grad = shared[2 * slot_count + local_blocks :].reshape(local_blocks * piece, 128)
    return result, input_grad, up_grad, down_grad, ends[0], up_right_grad, down_left_grad, ends[1]


def solution(mesh):
    return jax.shard_map(
        shards,
        mesh=mesh,
        in_specs=(
            P("dp", "tensor"),
            P("dp", "tensor"),
            P("tensor", None, None),
            P("tensor", None, None),
            P("tensor", None),
            P(None, "tensor"),
            P("tensor", None),
            P(None, "tensor"),
            P("tensor"),
            P("tensor"),
            P("tensor"),
        ),
        out_specs=(
            P("dp", "tensor"),
            P("dp", "tensor"),
            P("tensor", "dp", None),
            P("tensor", "dp", None),
            P(("tensor", "dp"), None),
            P("dp", "tensor"),
            P(("tensor", "dp"), None),
            P("dp", "tensor"),
        ),
        check_vma=False,
    )
```

```python
import jax
import jax.numpy as jnp
from jax import lax
from jax.experimental import pallas as pl
from jax.experimental.pallas import tpu as pltpu
from jax.sharding import PartitionSpec as P

f32 = jnp.float32
highest = lax.Precision.HIGHEST
VMEM = pl.BlockSpec(memory_space=pltpu.VMEM)
HBM = pl.BlockSpec(memory_space=pl.ANY)
SMEM = pl.BlockSpec(memory_space=pltpu.SMEM)
PARAMS = pltpu.CompilerParams(vmem_limit_bytes=48 * 1024 * 1024)
ROOT = 0.7978845608028654
CUBE = 0.044715
BATCH = 4

NN = ((1,), (0,))
NT = ((1,), (1,))
TN = ((0,), (0,))


def split(value):
    high = value.astype(jnp.bfloat16)
    return high, (value - high.astype(f32)).astype(jnp.bfloat16)


def dot3(left, right, dims):
    def one(a, b):
        return lax.dot_general(a, b, (dims, ((), ())), preferred_element_type=f32)

    return one(left[0], right[0]) + (one(left[0], right[1]) + one(left[1], right[0]))


def load(pairs, sems):
    copies = [pltpu.make_async_copy(a, b, sems.at[i]) for i, (a, b) in enumerate(pairs)]
    for copy in copies:
        copy.start()
    return copies


def grads_kernel(
    model_ref, hidden_ref, live_ref, group_ref, fields_hbm, up_hbm, down_hbm, low_ref, right_ref, left_ref,
    keep_up_ref, send_up_ref, keep_down_ref, send_down_ref, act_ref, pgrad_ref,
    fields_ref, up_ref, down_ref, square_ref, tall_ref, sems,
):
    rows = act_ref.shape[1]
    local_blocks = act_ref.shape[0]
    slot_count = up_ref.shape[0]
    piece = keep_up_ref.shape[3]
    copies = load([(fields_hbm, fields_ref), (up_hbm, up_ref), (down_hbm, down_ref)], sems)
    live = live_ref[0]
    group = group_ref[0]
    low_in = split(low_ref[0:rows])
    back_mid = split(low_ref[rows : 2 * rows])

    def deal(keep_ref, send_ref, near, tile, source, stride, start):
        homes = {0: (keep_ref, 0), near ^ 2: (keep_ref, 1), near: (send_ref, 0), 2: (send_ref, 1)}
        for rel in range(8):
            ref, at = homes[rel >> 1]
            first = pl.multiple_of((group ^ rel) * stride + start, piece)
            ref[at, rel & 1, tile] = source[pl.ds(first, piece)]

    for h in range(local_blocks):
        span = slice(h * 128, (h + 1) * 128)
        act_ref[h] = dot3(low_in, split(right_ref[:, span]), NN)
        pgrad_ref[h] = dot3(back_mid, split(left_ref[span]), NT)
    for copy in copies:
        copy.wait()

    @pl.loop(0, slot_count // BATCH)
    def _(step):
        terms = []
        for j in range(BATCH):
            s = step * BATCH + j
            m = model_ref[s]
            alive = jnp.where(s < live, 1.0, 0.0).astype(f32)
            up = dot3(split(fields_ref[m, 0:rows]), split(up_ref[s]), NN)
            back = dot3(split(fields_ref[m, rows : 2 * rows]), split(down_ref[s]), NT)
            terms.append((hidden_ref[s], up * alive, back * alive))
        for h, up, back in terms:
            act_ref[h] += up
            pgrad_ref[h] += back

    for h in range(local_blocks):
        value = act_ref[h]
        square = value * value
        bent = jnp.tanh(ROOT * (value + CUBE * (value * square)))
        half = 0.5 * (1.0 + bent)
        slope = half + 0.5 * value * (1.0 - bent * bent) * (ROOT * (1.0 + 3.0 * CUBE * square))
        hidden = value * half
        pgrad = pgrad_ref[h] * slope
        act_ref[h] = hidden
        pgrad_ref[h] = pgrad
        square_ref[h] = dot3(low_in, split(pgrad), TN)
        deal(keep_up_ref, send_up_ref, 1, slot_count + h, square_ref.at[h], piece, 0)
        tall_ref[h * 128 : (h + 1) * 128] = dot3(split(hidden), back_mid, TN)
    for i in range(local_blocks):
        deal(keep_down_ref, send_down_ref, 3, slot_count + i, tall_ref, piece * local_blocks, piece * i)

    @pl.loop(0, slot_count // BATCH)
    def _(step):
        for j in range(BATCH):
            s = step * BATCH + j
            m = model_ref[s]
            h = hidden_ref[s]
            alive = jnp.where(s < live, 1.0, 0.0).astype(f32)
            square_ref[2 * j] = dot3(split(fields_ref[m, 0:rows]), split(pgrad_ref[h]), TN) * alive
            square_ref[2 * j + 1] = dot3(split(act_ref[h]), split(fields_ref[m, rows : 2 * rows]), TN) * alive
        for j in range(BATCH):
            s = step * BATCH + j
            deal(keep_up_ref, send_up_ref, 1, s, square_ref.at[2 * j], piece, 0)
            deal(keep_down_ref, send_down_ref, 3, s, square_ref.at[2 * j + 1], piece, 0)


def terms_kernel(
    place_ref, hidden_ref, live_ref, up_hbm, down_hbm, act_ref, pgrad_ref, right_ref, left_ref,
    keep_ref, send_ref, up_ref, down_ref, sums, sems,
):
    rows = act_ref.shape[1]
    local_blocks = act_ref.shape[0]
    slot_count = up_ref.shape[0]
    copies = load([(up_hbm, up_ref), (down_hbm, down_ref)], sems)
    live = live_ref[0]
    low_mid = None
    back_in = None
    for h in range(local_blocks):
        span = slice(h * 128, (h + 1) * 128)
        mid = dot3(split(act_ref[h]), split(left_ref[span]), NN)
        back = dot3(split(pgrad_ref[h]), split(right_ref[:, span]), NT)
        low_mid = mid if low_mid is None else low_mid + mid
        back_in = back if back_in is None else back_in + back
    for ref in (keep_ref, send_ref):
        ref[0, 8] = low_mid
        ref[1, 8] = back_in
    for p in range(2):
        for b in range(16):
            sums[p, b] = jnp.zeros((rows, 128), f32)
    for copy in copies:
        copy.wait()

    @pl.loop(0, slot_count // BATCH)
    def _(step):
        terms = []
        for j in range(BATCH):
            s = step * BATCH + j
            h = hidden_ref[s]
            alive = jnp.where(s < live, 1.0, 0.0).astype(f32)
            out = dot3(split(act_ref[h]), split(down_ref[s]), NN) * alive
            back = dot3(split(pgrad_ref[h]), split(up_ref[s]), NT) * alive
            terms.append((place_ref[s], out, back))
        for b, out, back in terms:
            sums[0, b] += out
            sums[1, b] += back

    keep_ref[:, 0:8] = sums[:, 0:8]
    send_ref[:, 0:8] = sums[:, 8:16]


def xor_shift(value, bits, axis="tensor"):
    return lax.ppermute(value, axis, [(i, i ^ bits) for i in range(lax.axis_size(axis))])


def exchange(value):
    return lax.all_to_all(value, "tensor", 0, 0, tiled=True)


def low_total(partial_value):
    size = lax.axis_size("tensor")
    pieces = exchange(partial_value.reshape(size, -1, 128)).sum(axis=0)
    spread = exchange(jnp.broadcast_to(pieces[None], (size,) + pieces.shape))
    return spread.reshape(partial_value.shape)


def block_total(keep, send, core, x, z):
    other = xor_shift(send, 1)
    mine = ((x // 2) ^ core) == 0

    def merged(part):
        own, got = keep[part], other[part]
        zero = own[0:4] + got[0:4]
        rest = []
        for at in (4, 6):
            a, b = own[at : at + 2], got[at : at + 2]
            rest.append(jnp.concatenate([jnp.where(mine, a, b), jnp.where(mine, b, a)]))
        return jnp.stack([zero] + rest), own[8] + got[8]

    def along_x(terms, low, near, far):
        mix = near ^ far
        got = xor_shift(jnp.concatenate([terms[:, near], terms[:, mix], low[None]]), near << 1)

        def value(f, pair, e):
            total = terms[f, e] if f < 3 else None
            if (f ^ near) < 3:
                add = got[3 * pair + (f ^ near)]
                total = add if total is None else total + add
            return total

        low = low + got[6]
        more = xor_shift(jnp.stack([value(f, 1, far) for f in range(4)] + [low]), far << 1)
        return jnp.stack([value(f, 0, 0) + more[f ^ far] for f in range(4)]), low + more[4]

    out, low_mid = along_x(*merged(0), 1, 3)
    back, back_in = along_x(*merged(1), 3, 1)
    both = jnp.stack([out, back], axis=1)
    lows = jnp.stack([low_mid, back_in])
    w = x ^ z
    pick = lambda at: lax.dynamic_index_in_dim(both, at, 0, keepdims=False)
    got = xor_shift(jnp.stack([pick(w ^ 1), pick(w ^ 3), lows]), 1 << 3)
    lows = lows + got[2]
    last = xor_shift(jnp.stack([pick(w ^ 2) + got[1], lows]), 2 << 3)
    return pick(w) + got[0] + last[0], lows + last[1]


def group_sums(keep, send, near):
    far = near ^ 2
    got = xor_shift(send, near << 1, "dp")
    more = xor_shift(keep[1] + got[1], far << 1, "dp")
    return lambda z_hi: keep[0, z_hi] + got[0, z_hi] + more[z_hi]


def shards(
    inputs, out_grad, up_weight, down_weight, up_left, up_right, down_left, down_right,
    model_block, hidden_block, live_slots,
):
    rows = inputs.shape[0]
    slot_count = up_weight.shape[0]
    local_blocks = up_right.shape[1] // 128
    parts = lax.axis_size("dp")
    piece = 128 // parts
    me = lax.axis_index("tensor").astype(jnp.int32)
    core, x, z = me & 1, (me >> 1) & 3, me >> 3
    e = ((model_block >> 1) & 3) ^ x
    zrel = (model_block >> 3) ^ x
    place = jnp.where(zrel == 0, e, 2 + 2 * zrel + (e & 1)) + 8 * ((model_block & 1) ^ core)

    fields = lax.all_gather(jnp.concatenate([inputs, out_grad]), "tensor")
    low = low_total(
        jnp.concatenate(
            [
                jnp.dot(inputs, up_left, precision=highest),
                lax.dot_general(out_grad, down_right, (NT, ((), ())), precision=highest),
            ]
        )
    )
    group = lax.axis_index("dp").astype(jnp.int32)[None]
    tiles = slot_count + local_blocks
    dealt = jax.ShapeDtypeStruct((2, 2, tiles, piece, 128), f32)
    local = jax.ShapeDtypeStruct((local_blocks, rows, 128), f32)
    keep_up, send_up, keep_down, send_down, act, pgrad = pl.pallas_call(
        grads_kernel,
        out_shape=(dealt,) * 4 + (local,) * 2,
        in_specs=[SMEM] * 4 + [HBM] * 3 + [VMEM] * 3,
        out_specs=(VMEM,) * 6,
        scratch_shapes=[
            pltpu.VMEM(fields.shape, f32),
            pltpu.VMEM(up_weight.shape, f32),
            pltpu.VMEM(down_weight.shape, f32),
            pltpu.VMEM((2 * BATCH, 128, 128), f32),
            pltpu.VMEM(down_left.shape, f32),
            pltpu.SemaphoreType.DMA((3,)),
        ],
        compiler_params=PARAMS,
        cost_estimate=pl.CostEstimate(flops=3 * 10**9, bytes_accessed=12 * 10**6, transcendentals=0),
        name="grads",
    )(model_block, hidden_block, live_slots, group, fields, up_weight, down_weight, low, up_right, down_left)
    up_sum = group_sums(keep_up, send_up, 1)
    down_sum = group_sums(keep_down, send_down, 3)
    keep, send = pl.pallas_call(
        terms_kernel,
        out_shape=(jax.ShapeDtypeStruct((2, 9, rows, 128), f32),) * 2,
        in_specs=[SMEM] * 3 + [HBM] * 2 + [VMEM] * 4,
        out_specs=(VMEM,) * 2,
        scratch_shapes=[
            pltpu.VMEM(up_weight.shape, f32),
            pltpu.VMEM(down_weight.shape, f32),
            pltpu.VMEM((2, 16, rows, 128), f32),
            pltpu.SemaphoreType.DMA((2,)),
        ],
        compiler_params=PARAMS,
        cost_estimate=pl.CostEstimate(flops=15 * 10**8, bytes_accessed=6 * 10**6, transcendentals=0),
        name="terms",
    )(place, hidden_block, live_slots, up_weight, down_weight, act, pgrad, up_right, down_left)
    blocks, lows = block_total(keep, send, core, x, z)
    last = xor_shift(jnp.stack([up_sum(1), down_sum(1)]), 1, "dp")
    up_shared = up_sum(0) + last[0]
    down_shared = down_sum(0) + last[1]
    low_mid, back_in = lows[0], lows[1]
    left_part = lax.dot_general(inputs, back_in, (TN, ((), ())), precision=highest)
    right_part = lax.dot_general(low_mid, out_grad, (TN, ((), ())), precision=highest)
    ends = jnp.stack([left_part.reshape(parts, piece, 128), right_part.reshape(parts, piece, 128)], axis=1)
    ends = lax.all_to_all(ends, "dp", 0, 0, tiled=True).sum(axis=0)
    result = blocks[0] + jnp.dot(low_mid, down_right, precision=highest)
    input_grad = blocks[1] + lax.dot_general(back_in, up_left, (NT, ((), ())), precision=highest)
    up_right_grad = up_shared[slot_count:].transpose(1, 0, 2).reshape(piece, local_blocks * 128)
    down_left_grad = down_shared[slot_count:].reshape(local_blocks * piece, 128)
    return (
        result, input_grad, up_shared[:slot_count], down_shared[:slot_count],
        ends[0], up_right_grad, down_left_grad, ends[1],
    )


def solution(mesh):
    return jax.shard_map(
        shards,
        mesh=mesh,
        in_specs=(
            P("dp", "tensor"),
            P("dp", "tensor"),
            P("tensor", None, None),
            P("tensor", None, None),
            P("tensor", None),
            P(None, "tensor"),
            P("tensor", None),
            P(None, "tensor"),
            P("tensor"),
            P("tensor"),
            P("tensor"),
        ),
        out_specs=(
            P("dp", "tensor"),
            P("dp", "tensor"),
            P("tensor", "dp", None),
            P("tensor", "dp", None),
            P(("tensor", "dp"), None),
            P("dp", "tensor"),
            P(("tensor", "dp"), None),
            P("dp", "tensor"),
        ),
        check_vma=False,
    )
```

```python
import jax
import jax.numpy as jnp
from jax import lax
from jax.experimental import pallas as pl
from jax.experimental.pallas import tpu as pltpu
from jax.sharding import PartitionSpec as P

f32 = jnp.float32
highest = lax.Precision.HIGHEST
VMEM = pl.BlockSpec(memory_space=pltpu.VMEM)
HBM = pl.BlockSpec(memory_space=pl.ANY)
SMEM = pl.BlockSpec(memory_space=pltpu.SMEM)
ROOT = 0.7978845608028654
CUBE = 0.044715
BATCH = 4

NN = ((1,), (0,))
NT = ((1,), (1,))
TN = ((0,), (0,))


def split(value):
    high = value.astype(jnp.bfloat16)
    return high, (value - high.astype(f32)).astype(jnp.bfloat16)


def dot3(left, right, dims):
    def one(a, b):
        return lax.dot_general(a, b, (dims, ((), ())), preferred_element_type=f32)

    return one(left[0], right[0]) + (one(left[0], right[1]) + one(left[1], right[0]))


def load(pairs, sems):
    copies = [pltpu.make_async_copy(a, b, sems.at[i]) for i, (a, b) in enumerate(pairs)]
    for copy in copies:
        copy.start()
    return copies


def hidden_kernel(
    model_ref, hidden_ref, live_ref, fields_hbm, up_hbm, down_hbm, low_ref, right_ref, left_ref,
    act_ref, pgrad_ref, part_ref, fields_ref, up_ref, down_ref, sems,
):
    rows = act_ref.shape[1]
    local_blocks = act_ref.shape[0]
    slot_count = up_ref.shape[0]
    copies = load([(fields_hbm, fields_ref), (up_hbm, up_ref), (down_hbm, down_ref)], sems)
    live = live_ref[0]
    low_in = split(low_ref[0:rows])
    back_mid = split(low_ref[rows : 2 * rows])
    for h in range(local_blocks):
        span = slice(h * 128, (h + 1) * 128)
        act_ref[h] = dot3(low_in, split(right_ref[:, span]), NN)
        pgrad_ref[h] = dot3(back_mid, split(left_ref[span]), NT)
    for copy in copies:
        copy.wait()

    @pl.loop(0, slot_count // BATCH)
    def _(step):
        terms = []
        for j in range(BATCH):
            s = step * BATCH + j
            m = model_ref[s]
            alive = jnp.where(s < live, 1.0, 0.0).astype(f32)
            up = dot3(split(fields_ref[m, 0:rows]), split(up_ref[s]), NN)
            back = dot3(split(fields_ref[m, rows : 2 * rows]), split(down_ref[s]), NT)
            terms.append((hidden_ref[s], up * alive, back * alive))
        for h, up, back in terms:
            act_ref[h] += up
            pgrad_ref[h] += back

    low_mid = None
    back_in = None
    for h in range(local_blocks):
        value = act_ref[h]
        square = value * value
        bent = jnp.tanh(ROOT * (value + CUBE * (value * square)))
        half = 0.5 * (1.0 + bent)
        slope = half + 0.5 * value * (1.0 - bent * bent) * (ROOT * (1.0 + 3.0 * CUBE * square))
        hidden = value * half
        pgrad = pgrad_ref[h] * slope
        act_ref[h] = hidden
        pgrad_ref[h] = pgrad
        span = slice(h * 128, (h + 1) * 128)
        mid = dot3(split(hidden), split(left_ref[span]), NN)
        back = dot3(split(pgrad), split(right_ref[:, span]), NT)
        low_mid = mid if low_mid is None else low_mid + mid
        back_in = back if back_in is None else back_in + back
    part_ref[0:rows] = low_mid
    part_ref[rows : 2 * rows] = back_in


def grads_kernel(
    model_ref, hidden_ref, live_ref, group_ref, fields_hbm, after_hbm, act_ref, pgrad_ref, low_ref,
    keep_up_ref, send_up_ref, keep_down_ref, send_down_ref, fields_ref, square_ref, tall_ref, sems,
):
    rows = act_ref.shape[1]
    local_blocks = act_ref.shape[0]
    slot_count = model_ref.shape[0]
    piece = keep_up_ref.shape[3]
    copies = load([(fields_hbm, fields_ref)], sems)
    live = live_ref[0]
    group = group_ref[0]
    low_in = split(low_ref[0:rows])
    back_mid = split(low_ref[rows : 2 * rows])

    def deal(keep_ref, send_ref, near, tile, source, stride, start):
        homes = {0: (keep_ref, 0), near ^ 2: (keep_ref, 1), near: (send_ref, 0), 2: (send_ref, 1)}
        for rel in range(8):
            ref, at = homes[rel >> 1]
            first = pl.multiple_of((group ^ rel) * stride + start, piece)
            ref[at, rel & 1, tile] = source[pl.ds(first, piece)]

    for h in range(local_blocks):
        square_ref[h] = dot3(low_in, split(pgrad_ref[h]), TN)
        deal(keep_up_ref, send_up_ref, 1, slot_count + h, square_ref.at[h], piece, 0)
        tall_ref[h * 128 : (h + 1) * 128] = dot3(split(act_ref[h]), back_mid, TN)
    for i in range(local_blocks):
        deal(keep_down_ref, send_down_ref, 3, slot_count + i, tall_ref, piece * local_blocks, piece * i)
    for copy in copies:
        copy.wait()

    @pl.loop(0, slot_count // BATCH)
    def _(step):
        for j in range(BATCH):
            s = step * BATCH + j
            m = model_ref[s]
            h = hidden_ref[s]
            alive = jnp.where(s < live, 1.0, 0.0).astype(f32)
            square_ref[2 * j] = dot3(split(fields_ref[m, 0:rows]), split(pgrad_ref[h]), TN) * alive
            square_ref[2 * j + 1] = dot3(split(act_ref[h]), split(fields_ref[m, rows : 2 * rows]), TN) * alive
        for j in range(BATCH):
            s = step * BATCH + j
            deal(keep_up_ref, send_up_ref, 1, s, square_ref.at[2 * j], piece, 0)
            deal(keep_down_ref, send_down_ref, 3, s, square_ref.at[2 * j + 1], piece, 0)


def terms_kernel(
    place_ref, hidden_ref, live_ref, up_hbm, down_hbm, act_ref, pgrad_ref,
    keep_ref, send_ref, up_ref, down_ref, sums, sems,
):
    rows = act_ref.shape[1]
    slot_count = up_ref.shape[0]
    copies = load([(up_hbm, up_ref), (down_hbm, down_ref)], sems)
    live = live_ref[0]
    for p in range(2):
        for b in range(16):
            sums[p, b] = jnp.zeros((rows, 128), f32)
    for copy in copies:
        copy.wait()

    @pl.loop(0, slot_count // BATCH)
    def _(step):
        terms = []
        for j in range(BATCH):
            s = step * BATCH + j
            h = hidden_ref[s]
            alive = jnp.where(s < live, 1.0, 0.0).astype(f32)
            out = dot3(split(act_ref[h]), split(down_ref[s]), NN) * alive
            back = dot3(split(pgrad_ref[h]), split(up_ref[s]), NT) * alive
            terms.append((place_ref[s], out, back))
        for b, out, back in terms:
            sums[0, b] += out
            sums[1, b] += back

    keep_ref[...] = sums[:, 0:8]
    send_ref[...] = sums[:, 8:16]


NEAR = (1, 3)


def core_kernel(first_ref, keep_ref, other_ref, hold_ref, send_out_ref, send_back_ref):
    first = first_ref[0]
    for p, send_ref in enumerate((send_out_ref, send_back_ref)):
        near = NEAR[p]
        homes = {0: (hold_ref.at[p], 0), near ^ 2: (hold_ref.at[p], 3), near: (send_ref, 0), 2: (send_ref, 3)}
        for e in range(4):
            ref, at = homes[e]
            ref[at] = keep_ref[p, e] + other_ref[p, e]
            mine = jnp.where(first == (e >> 1), 1.0, 0.0).astype(f32)
            for i in (1, 2):
                b = 2 + 2 * i + (e & 1)
                ref[at + i] = keep_ref[p, b] * mine + other_ref[p, b] * (1.0 - mine)


def near_kernel(hold_ref, got_out_ref, got_back_ref, stay_ref, send_out_ref, send_back_ref):
    for p, (got_ref, send_ref) in enumerate(((got_out_ref, send_out_ref), (got_back_ref, send_back_ref))):
        for f in range(4):
            for pair in range(2):
                total = hold_ref[p, 3 * pair + f] if f < 3 else None
                g = f ^ NEAR[p]
                if g < 3:
                    add = got_ref[3 * pair + g]
                    total = add if total is None else total + add
                if pair:
                    send_ref[f] = total
                else:
                    stay_ref[p, f] = total


def far_kernel(w_ref, stay_ref, got_out_ref, got_back_ref, hold_ref, send_ref):
    w = w_ref[0]
    for flip, ref, at in ((0, hold_ref, 0), (2, hold_ref, 1), (1, send_ref, 0), (3, send_ref, 1)):
        f = w ^ flip
        for p, got_ref in enumerate((got_out_ref, got_back_ref)):
            ref[at, p] = stay_ref[p, f] + got_ref[f ^ (NEAR[p] ^ 2)]


def y_kernel(keep_up_ref, got_up_ref, keep_down_ref, got_down_ref, after_hbm, hold_ref, send_up_ref, send_down_ref):
    hold_ref[0] = keep_up_ref[0] + got_up_ref[0]
    hold_ref[1] = keep_down_ref[0] + got_down_ref[0]
    send_up_ref[...] = keep_up_ref[1] + got_up_ref[1]
    send_down_ref[...] = keep_down_ref[1] + got_down_ref[1]


def ring_kernel(hold_ref, got_up_ref, got_down_ref, after_hbm, stay_ref, send_ref):
    for p, got_ref in enumerate((got_up_ref, got_down_ref)):
        stay_ref[p] = hold_ref[p, 0] + got_ref[0]
        send_ref[p] = hold_ref[p, 1] + got_ref[1]


def last_kernel(stay_ref, got_ref, up_ref, right_ref, down_ref, left_ref):
    slot_count, piece, _ = up_ref.shape
    up_ref[...] = stay_ref[0, 0:slot_count] + got_ref[0, 0:slot_count]
    down_ref[...] = stay_ref[1, 0:slot_count] + got_ref[1, 0:slot_count]
    for h in range(right_ref.shape[1] // 128):
        right_ref[:, h * 128 : (h + 1) * 128] = stay_ref[0, slot_count + h] + got_ref[0, slot_count + h]
        left_ref[h * piece : (h + 1) * piece] = stay_ref[1, slot_count + h] + got_ref[1, slot_count + h]


def call(kernel, name, in_specs, outs, scratch=(), mflops=1, kbytes=1000):
    limit = (48 if scratch else 24) * 1024 * 1024
    return pl.pallas_call(
        kernel,
        out_shape=tuple(jax.ShapeDtypeStruct(shape, f32) for shape in outs),
        in_specs=in_specs,
        out_specs=(VMEM,) * len(outs),
        scratch_shapes=list(scratch),
        compiler_params=pltpu.CompilerParams(vmem_limit_bytes=limit),
        cost_estimate=pl.CostEstimate(flops=mflops * 10**6, bytes_accessed=kbytes * 10**3, transcendentals=0),
        name=name,
    )


def xor_shift(value, bits, axis="tensor"):
    return lax.ppermute(value, axis, [(i, i ^ bits) for i in range(lax.axis_size(axis))])


def exchange(value):
    return lax.all_to_all(value, "tensor", 0, 0, tiled=True)


def low_pieces(partial_value):
    size = lax.axis_size("tensor")
    return exchange(partial_value.reshape(size, -1, 128)).sum(axis=0)


def low_whole(pieces):
    size = lax.axis_size("tensor")
    return exchange(jnp.broadcast_to(pieces[None], (size,) + pieces.shape)).reshape(-1, 128)


def shards(
    inputs, out_grad, up_weight, down_weight, up_left, up_right, down_left, down_right,
    model_block, hidden_block, live_slots,
):
    rows = inputs.shape[0]
    slot_count = up_weight.shape[0]
    local_blocks = up_right.shape[1] // 128
    parts = lax.axis_size("dp")
    piece = 128 // parts
    me = lax.axis_index("tensor").astype(jnp.int32)
    core, x, z = me & 1, (me >> 1) & 3, me >> 3
    e = ((model_block >> 1) & 3) ^ x
    zrel = (model_block >> 3) ^ x
    place = jnp.where(zrel == 0, e, 2 + 2 * zrel + (e & 1)) + 8 * ((model_block & 1) ^ core)

    fields = lax.all_gather(jnp.concatenate([inputs, out_grad]), "tensor")
    first_part = jnp.concatenate(
        [
            jnp.dot(inputs, up_left, precision=highest),
            lax.dot_general(out_grad, down_right, (NT, ((), ())), precision=highest),
        ]
    )
    low = low_whole(low_pieces(first_part))
    group = lax.axis_index("dp").astype(jnp.int32)[None]
    local = (local_blocks, rows, 128)
    act, pgrad, low_part = call(
        hidden_kernel,
        "hidden",
        [SMEM] * 3 + [HBM] * 3 + [VMEM] * 3,
        (local, local, (2 * rows, 128)),
        [
            pltpu.VMEM(fields.shape, f32),
            pltpu.VMEM(up_weight.shape, f32),
            pltpu.VMEM(down_weight.shape, f32),
            pltpu.SemaphoreType.DMA((3,)),
        ],
        2000,
        12000,
    )(model_block, hidden_block, live_slots, fields, up_weight, down_weight, low, up_right, down_left)
    pieces = low_pieces(low_part)
    keep, send = call(
        terms_kernel,
        "terms",
        [SMEM] * 3 + [HBM] * 2 + [VMEM] * 2,
        ((2, 8, rows, 128),) * 2,
        [
            pltpu.VMEM(up_weight.shape, f32),
            pltpu.VMEM(down_weight.shape, f32),
            pltpu.VMEM((2, 16, rows, 128), f32),
            pltpu.SemaphoreType.DMA((2,)),
        ],
        1500,
        12000,
    )(place, hidden_block, live_slots, up_weight, down_weight, act, pgrad)
    other = xor_shift(send, 1)
    hold, send_out, send_back = call(
        core_kernel, "core", [SMEM] + [VMEM] * 2, ((2, 6, rows, 128), (6, rows, 128), (6, rows, 128))
    )(((x // 2) ^ core)[None], keep, other)
    tiles = slot_count + local_blocks
    keep_up, send_up, keep_down, send_down = call(
        grads_kernel,
        "grads",
        [SMEM] * 4 + [HBM] * 2 + [VMEM] * 3,
        ((2, 2, tiles, piece, 128),) * 4,
        [
            pltpu.VMEM(fields.shape, f32),
            pltpu.VMEM((2 * BATCH, 128, 128), f32),
            pltpu.VMEM(down_left.shape, f32),
            pltpu.SemaphoreType.DMA((1,)),
        ],
        1500,
        12000,
    )(model_block, hidden_block, live_slots, group, fields, send_out, act, pgrad, low)
    got_out = xor_shift(send_out, NEAR[0] << 1)
    got_back = xor_shift(send_back, NEAR[1] << 1)
    got_up = xor_shift(send_up, NEAR[0] << 1, "dp")
    got_down = xor_shift(send_down, NEAR[1] << 1, "dp")
    stay, send_out, send_back = call(
        near_kernel, "near", [VMEM] * 3, ((2, 4, rows, 128), (4, rows, 128), (4, rows, 128))
    )(hold, got_out, got_back)
    got_out = xor_shift(send_out, NEAR[1] << 1)
    got_back = xor_shift(send_back, NEAR[0] << 1)
    pair = (2, 2, rows, 128)
    hold, send = call(far_kernel, "far", [SMEM] + [VMEM] * 3, (pair, pair))((x ^ z)[None], stay, got_out, got_back)
    got = xor_shift(send, 1 << 3)
    half = (2, tiles, piece, 128)
    hold_grads, send_up, send_down = call(
        y_kernel, "ring_y", [VMEM] * 4 + [HBM], ((2,) + half, half, half)
    )(keep_up, got_up, keep_down, got_down, send)
    got_up = xor_shift(send_up, NEAR[1] << 1, "dp")
    got_down = xor_shift(send_down, NEAR[0] << 1, "dp")
    near_z = hold[0] + got[0]
    send = hold[1] + got[1]
    blocks = near_z + xor_shift(send, 2 << 3)
    stay_grads, send = call(ring_kernel, "ring_far", [VMEM] * 3 + [HBM], (half, half))(
        hold_grads, got_up, got_down, send
    )
    up_grad, up_right_grad, down_grad, down_left_grad = call(
        last_kernel,
        "last",
        [VMEM] * 2,
        ((slot_count, piece, 128), (piece, local_blocks * 128), (slot_count, piece, 128), (local_blocks * piece, 128)),
    )(stay_grads, xor_shift(send, 1, "dp"))
    lows = low_whole(pieces)
    low_mid, back_in = lows[:rows], lows[rows:]
    left_part = lax.dot_general(inputs, back_in, (TN, ((), ())), precision=highest)
    right_part = lax.dot_general(low_mid, out_grad, (TN, ((), ())), precision=highest)
    ends = jnp.stack([left_part.reshape(parts, piece, 128), right_part.reshape(parts, piece, 128)], axis=1)
    ends = lax.all_to_all(ends, "dp", 0, 0, tiled=True).sum(axis=0)
    result = blocks[0] + jnp.dot(low_mid, down_right, precision=highest)
    input_grad = blocks[1] + lax.dot_general(back_in, up_left, (NT, ((), ())), precision=highest)
    return result, input_grad, up_grad, down_grad, ends[0], up_right_grad, down_left_grad, ends[1]


def solution(mesh):
    return jax.shard_map(
        shards,
        mesh=mesh,
        in_specs=(
            P("dp", "tensor"),
            P("dp", "tensor"),
            P("tensor", None, None),
            P("tensor", None, None),
            P("tensor", None),
            P(None, "tensor"),
            P("tensor", None),
            P(None, "tensor"),
            P("tensor"),
            P("tensor"),
            P("tensor"),
        ),
        out_specs=(
            P("dp", "tensor"),
            P("dp", "tensor"),
            P("tensor", "dp", None),
            P("tensor", "dp", None),
            P(("tensor", "dp"), None),
            P("dp", "tensor"),
            P(("tensor", "dp"), None),
            P("dp", "tensor"),
        ),
        check_vma=False,
    )
```

```python
import jax
import jax.numpy as jnp
from jax import lax
from jax.experimental import pallas as pl
from jax.experimental.pallas import tpu as pltpu
from jax.sharding import PartitionSpec as P

f32 = jnp.float32
highest = lax.Precision.HIGHEST
VMEM = pl.BlockSpec(memory_space=pltpu.VMEM)
HBM = pl.BlockSpec(memory_space=pl.ANY)
SMEM = pl.BlockSpec(memory_space=pltpu.SMEM)
ROOT = 0.7978845608028654
CUBE = 0.044715
BATCH = 4

NN = ((1,), (0,))
NT = ((1,), (1,))
TN = ((0,), (0,))


def split(value):
    high = value.astype(jnp.bfloat16)
    return high, (value - high.astype(f32)).astype(jnp.bfloat16)


def dot3(left, right, dims):
    def one(a, b):
        return lax.dot_general(a, b, (dims, ((), ())), preferred_element_type=f32)

    return one(left[0], right[0]) + (one(left[0], right[1]) + one(left[1], right[0]))


def load(pairs, sems):
    copies = [pltpu.make_async_copy(a, b, sems.at[i]) for i, (a, b) in enumerate(pairs)]
    for copy in copies:
        copy.start()
    return copies


def hidden_kernel(
    model_ref, hidden_ref, live_ref, fields_hbm, up_hbm, down_hbm, low_ref, right_ref, left_ref,
    act_ref, pgrad_ref, part_ref, fields_ref, up_ref, down_ref, sems,
):
    rows = act_ref.shape[1]
    local_blocks = act_ref.shape[0]
    slot_count = up_ref.shape[0]
    copies = load([(fields_hbm, fields_ref), (up_hbm, up_ref), (down_hbm, down_ref)], sems)
    live = live_ref[0]
    low_in = split(low_ref[0:rows])
    back_mid = split(low_ref[rows : 2 * rows])
    for h in range(local_blocks):
        span = slice(h * 128, (h + 1) * 128)
        act_ref[h] = dot3(low_in, split(right_ref[:, span]), NN)
        pgrad_ref[h] = dot3(back_mid, split(left_ref[span]), NT)
    for copy in copies:
        copy.wait()

    @pl.loop(0, slot_count // BATCH)
    def _(step):
        terms = []
        for j in range(BATCH):
            s = step * BATCH + j
            m = model_ref[s]
            alive = jnp.where(s < live, 1.0, 0.0).astype(f32)
            up = dot3(split(fields_ref[m, 0:rows]), split(up_ref[s]), NN)
            back = dot3(split(fields_ref[m, rows : 2 * rows]), split(down_ref[s]), NT)
            terms.append((hidden_ref[s], up * alive, back * alive))
        for h, up, back in terms:
            act_ref[h] += up
            pgrad_ref[h] += back

    low_mid = None
    back_in = None
    for h in range(local_blocks):
        value = act_ref[h]
        square = value * value
        bent = jnp.tanh(ROOT * (value + CUBE * (value * square)))
        half = 0.5 * (1.0 + bent)
        slope = half + 0.5 * value * (1.0 - bent * bent) * (ROOT * (1.0 + 3.0 * CUBE * square))
        hidden = value * half
        pgrad = pgrad_ref[h] * slope
        act_ref[h] = hidden
        pgrad_ref[h] = pgrad
        span = slice(h * 128, (h + 1) * 128)
        mid = dot3(split(hidden), split(left_ref[span]), NN)
        back = dot3(split(pgrad), split(right_ref[:, span]), NT)
        low_mid = mid if low_mid is None else low_mid + mid
        back_in = back if back_in is None else back_in + back
    part_ref[0:rows] = low_mid
    part_ref[rows : 2 * rows] = back_in


def grads_kernel(
    model_ref, hidden_ref, live_ref, group_ref, fields_hbm, after_hbm, act_ref, pgrad_ref, low_ref,
    keep_up_ref, send_up_ref, keep_down_ref, send_down_ref, fields_ref, square_ref, tall_ref, sems,
):
    rows = act_ref.shape[1]
    local_blocks = act_ref.shape[0]
    slot_count = model_ref.shape[0]
    piece = keep_up_ref.shape[3]
    copies = load([(fields_hbm, fields_ref)], sems)
    live = live_ref[0]
    group = group_ref[0]
    low_in = split(low_ref[0:rows])
    back_mid = split(low_ref[rows : 2 * rows])

    def deal(keep_ref, send_ref, near, tile, source, stride, start):
        homes = {0: (keep_ref, 0), near ^ 2: (keep_ref, 1), near: (send_ref, 0), 2: (send_ref, 1)}
        for rel in range(8):
            ref, at = homes[rel >> 1]
            first = pl.multiple_of((group ^ rel) * stride + start, piece)
            ref[at, rel & 1, tile] = source[pl.ds(first, piece)]

    for h in range(local_blocks):
        square_ref[h] = dot3(low_in, split(pgrad_ref[h]), TN)
        deal(keep_up_ref, send_up_ref, 1, slot_count + h, square_ref.at[h], piece, 0)
        tall_ref[h * 128 : (h + 1) * 128] = dot3(split(act_ref[h]), back_mid, TN)
    for i in range(local_blocks):
        deal(keep_down_ref, send_down_ref, 3, slot_count + i, tall_ref, piece * local_blocks, piece * i)
    for copy in copies:
        copy.wait()

    @pl.loop(0, slot_count // BATCH)
    def _(step):
        for j in range(BATCH):
            s = step * BATCH + j
            m = model_ref[s]
            h = hidden_ref[s]
            alive = jnp.where(s < live, 1.0, 0.0).astype(f32)
            square_ref[2 * j] = dot3(split(fields_ref[m, 0:rows]), split(pgrad_ref[h]), TN) * alive
            square_ref[2 * j + 1] = dot3(split(act_ref[h]), split(fields_ref[m, rows : 2 * rows]), TN) * alive
        for j in range(BATCH):
            s = step * BATCH + j
            deal(keep_up_ref, send_up_ref, 1, s, square_ref.at[2 * j], piece, 0)
            deal(keep_down_ref, send_down_ref, 3, s, square_ref.at[2 * j + 1], piece, 0)


def terms_kernel(
    place_ref, hidden_ref, live_ref, up_hbm, down_hbm, act_ref, pgrad_ref,
    keep_ref, send_ref, up_ref, down_ref, sums, sems,
):
    rows = act_ref.shape[1]
    slot_count = up_ref.shape[0]
    copies = load([(up_hbm, up_ref), (down_hbm, down_ref)], sems)
    live = live_ref[0]
    for p in range(2):
        for b in range(16):
            sums[p, b] = jnp.zeros((rows, 128), f32)
    for copy in copies:
        copy.wait()

    @pl.loop(0, slot_count // BATCH)
    def _(step):
        terms = []
        for j in range(BATCH):
            s = step * BATCH + j
            h = hidden_ref[s]
            alive = jnp.where(s < live, 1.0, 0.0).astype(f32)
            out = dot3(split(act_ref[h]), split(down_ref[s]), NN) * alive
            back = dot3(split(pgrad_ref[h]), split(up_ref[s]), NT) * alive
            terms.append((place_ref[s], out, back))
        for b, out, back in terms:
            sums[0, b] += out
            sums[1, b] += back

    keep_ref[...] = sums[:, 0:8]
    send_ref[...] = sums[:, 8:16]


NEAR = (1, 3)


def core_kernel(first_ref, keep_ref, other_ref, hold_ref, send_out_ref, send_back_ref):
    first = first_ref[0]
    for p, send_ref in enumerate((send_out_ref, send_back_ref)):
        near = NEAR[p]
        homes = {0: (hold_ref.at[p], 0), near ^ 2: (hold_ref.at[p], 3), near: (send_ref, 0), 2: (send_ref, 3)}
        for e in range(4):
            ref, at = homes[e]
            ref[at] = keep_ref[p, e] + other_ref[p, e]
            mine = jnp.where(first == (e >> 1), 1.0, 0.0).astype(f32)
            for i in (1, 2):
                b = 2 + 2 * i + (e & 1)
                ref[at + i] = keep_ref[p, b] * mine + other_ref[p, b] * (1.0 - mine)


def near_kernel(hold_ref, got_out_ref, got_back_ref, stay_ref, send_out_ref, send_back_ref):
    for p, (got_ref, send_ref) in enumerate(((got_out_ref, send_out_ref), (got_back_ref, send_back_ref))):
        for f in range(4):
            for pair in range(2):
                total = hold_ref[p, 3 * pair + f] if f < 3 else None
                g = f ^ NEAR[p]
                if g < 3:
                    add = got_ref[3 * pair + g]
                    total = add if total is None else total + add
                if pair:
                    send_ref[f] = total
                else:
                    stay_ref[p, f] = total


def far_kernel(w_ref, stay_ref, got_out_ref, got_back_ref, hold_ref, send_ref):
    w = w_ref[0]
    for flip, ref, at in ((0, hold_ref, 0), (2, hold_ref, 1), (1, send_ref, 0), (3, send_ref, 1)):
        f = w ^ flip
        for p, got_ref in enumerate((got_out_ref, got_back_ref)):
            ref[at, p] = stay_ref[p, f] + got_ref[f ^ (NEAR[p] ^ 2)]


def y_kernel(keep_up_ref, got_up_ref, keep_down_ref, got_down_ref, after_hbm, hold_ref, send_up_ref, send_down_ref):
    hold_ref[0] = keep_up_ref[0] + got_up_ref[0]
    hold_ref[1] = keep_down_ref[0] + got_down_ref[0]
    send_up_ref[...] = keep_up_ref[1] + got_up_ref[1]
    send_down_ref[...] = keep_down_ref[1] + got_down_ref[1]


def ring_kernel(hold_ref, got_up_ref, got_down_ref, after_hbm, stay_ref, send_ref):
    for p, got_ref in enumerate((got_up_ref, got_down_ref)):
        stay_ref[p] = hold_ref[p, 0] + got_ref[0]
        send_ref[p] = hold_ref[p, 1] + got_ref[1]


def last_kernel(stay_ref, got_ref, up_ref, right_ref, down_ref, left_ref):
    slot_count, piece, _ = up_ref.shape
    up_ref[...] = stay_ref[0, 0:slot_count] + got_ref[0, 0:slot_count]
    down_ref[...] = stay_ref[1, 0:slot_count] + got_ref[1, 0:slot_count]
    for h in range(right_ref.shape[1] // 128):
        right_ref[:, h * 128 : (h + 1) * 128] = stay_ref[0, slot_count + h] + got_ref[0, slot_count + h]
        left_ref[h * piece : (h + 1) * piece] = stay_ref[1, slot_count + h] + got_ref[1, slot_count + h]


def ends_kernel(inputs_ref, grad_ref, low_ref, after_hbm, out_ref):
    parts, _, piece, _ = out_ref.shape
    rows = inputs_ref.shape[0]
    left = dot3(split(inputs_ref[...]), split(low_ref[rows : 2 * rows]), TN)
    right = dot3(split(low_ref[0:rows]), split(grad_ref[...]), TN)
    out_ref[:, 0] = left.reshape(parts, piece, 128)
    out_ref[:, 1] = right.reshape(parts, piece, 128)


def call(kernel, name, in_specs, outs, scratch=(), mflops=1, kbytes=1000):
    limit = (54 if name == "hidden" else 48 if scratch else 24) * 1024 * 1024
    return pl.pallas_call(
        kernel,
        out_shape=tuple(jax.ShapeDtypeStruct(shape, f32) for shape in outs),
        in_specs=in_specs,
        out_specs=(VMEM,) * len(outs),
        scratch_shapes=list(scratch),
        compiler_params=pltpu.CompilerParams(vmem_limit_bytes=limit),
        cost_estimate=pl.CostEstimate(flops=mflops * 10**6, bytes_accessed=kbytes * 10**3, transcendentals=0),
        name=name,
    )


def xor_shift(value, bits, axis="tensor"):
    return lax.ppermute(value, axis, [(i, i ^ bits) for i in range(lax.axis_size(axis))])


def exchange(value):
    return lax.all_to_all(value, "tensor", 0, 0, tiled=True)


def low_pieces(partial_value):
    size = lax.axis_size("tensor")
    return exchange(partial_value.reshape(size, -1, 128)).sum(axis=0)


def low_whole(pieces):
    size = lax.axis_size("tensor")
    return exchange(jnp.broadcast_to(pieces[None], (size,) + pieces.shape)).reshape(-1, 128)


def shards(
    inputs, out_grad, up_weight, down_weight, up_left, up_right, down_left, down_right,
    model_block, hidden_block, live_slots,
):
    rows = inputs.shape[0]
    slot_count = up_weight.shape[0]
    local_blocks = up_right.shape[1] // 128
    parts = lax.axis_size("dp")
    piece = 128 // parts
    me = lax.axis_index("tensor").astype(jnp.int32)
    core, x, z = me & 1, (me >> 1) & 3, me >> 3
    e = ((model_block >> 1) & 3) ^ x
    zrel = (model_block >> 3) ^ x
    place = jnp.where(zrel == 0, e, 2 + 2 * zrel + (e & 1)) + 8 * ((model_block & 1) ^ core)

    fields = lax.all_gather(jnp.concatenate([inputs, out_grad]), "tensor")
    first_part = jnp.concatenate(
        [
            jnp.dot(inputs, up_left, precision=highest),
            lax.dot_general(out_grad, down_right, (NT, ((), ())), precision=highest),
        ]
    )
    low = low_whole(low_pieces(first_part))
    group = lax.axis_index("dp").astype(jnp.int32)[None]
    local = (local_blocks, rows, 128)
    act, pgrad, low_part = call(
        hidden_kernel,
        "hidden",
        [SMEM] * 3 + [HBM] * 3 + [VMEM] * 3,
        (local, local, (2 * rows, 128)),
        [
            pltpu.VMEM(fields.shape, f32),
            pltpu.VMEM(up_weight.shape, f32),
            pltpu.VMEM(down_weight.shape, f32),
            pltpu.SemaphoreType.DMA((3,)),
        ],
        2000,
        12000,
    )(model_block, hidden_block, live_slots, fields, up_weight, down_weight, low, up_right, down_left)
    keep, send = call(
        terms_kernel,
        "terms",
        [SMEM] * 3 + [HBM] * 2 + [VMEM] * 2,
        ((2, 8, rows, 128),) * 2,
        [
            pltpu.VMEM(up_weight.shape, f32),
            pltpu.VMEM(down_weight.shape, f32),
            pltpu.VMEM((2, 16, rows, 128), f32),
            pltpu.SemaphoreType.DMA((2,)),
        ],
        1500,
        12000,
    )(place, hidden_block, live_slots, up_weight, down_weight, act, pgrad)
    tiles = slot_count + local_blocks
    keep_up, send_up, keep_down, send_down = call(
        grads_kernel,
        "grads",
        [SMEM] * 4 + [HBM] * 2 + [VMEM] * 3,
        ((2, 2, tiles, piece, 128),) * 4,
        [
            pltpu.VMEM(fields.shape, f32),
            pltpu.VMEM((2 * BATCH, 128, 128), f32),
            pltpu.VMEM(down_left.shape, f32),
            pltpu.SemaphoreType.DMA((1,)),
        ],
        1500,
        12000,
    )(model_block, hidden_block, live_slots, group, fields, send, act, pgrad, low)
    got_up = xor_shift(send_up, NEAR[0] << 1, "dp")
    got_down = xor_shift(send_down, NEAR[1] << 1, "dp")
    pieces = low_pieces(low_part)
    other = xor_shift(send, 1)
    hold, send_out, send_back = call(
        core_kernel, "core", [SMEM] + [VMEM] * 2, ((2, 6, rows, 128), (6, rows, 128), (6, rows, 128))
    )(((x // 2) ^ core)[None], keep, other)
    got_out = xor_shift(send_out, NEAR[0] << 1)
    got_back = xor_shift(send_back, NEAR[1] << 1)
    half = (2, tiles, piece, 128)
    hold_grads, send_up, send_down = call(
        y_kernel, "ring_y", [VMEM] * 4 + [HBM], ((2,) + half, half, half)
    )(keep_up, got_up, keep_down, got_down, send_out)
    got_up = xor_shift(send_up, NEAR[1] << 1, "dp")
    got_down = xor_shift(send_down, NEAR[0] << 1, "dp")
    stay, send_out, send_back = call(
        near_kernel, "near", [VMEM] * 3, ((2, 4, rows, 128), (4, rows, 128), (4, rows, 128))
    )(hold, got_out, got_back)
    got_out = xor_shift(send_out, NEAR[1] << 1)
    got_back = xor_shift(send_back, NEAR[0] << 1)
    pair = (2, 2, rows, 128)
    hold, send = call(far_kernel, "far", [SMEM] + [VMEM] * 3, (pair, pair))((x ^ z)[None], stay, got_out, got_back)
    got = xor_shift(send, 1 << 3)
    stay_grads, send_grads = call(ring_kernel, "ring_far", [VMEM] * 3 + [HBM], (half, half))(
        hold_grads, got_up, got_down, send
    )
    got_grads = xor_shift(send_grads, 1, "dp")
    blocks = hold[0] + got[0] + xor_shift(hold[1] + got[1], 2 << 3)
    lows = low_whole(pieces)
    low_mid, back_in = lows[:rows], lows[rows:]
    (ends,) = call(ends_kernel, "ends", [VMEM] * 3 + [HBM], ((parts, 2, piece, 128),))(
        inputs, out_grad, lows, send_grads
    )
    ends = lax.all_to_all(ends, "dp", 0, 0, tiled=True).sum(axis=0)
    up_grad, up_right_grad, down_grad, down_left_grad = call(
        last_kernel,
        "last",
        [VMEM] * 2,
        ((slot_count, piece, 128), (piece, local_blocks * 128), (slot_count, piece, 128), (local_blocks * piece, 128)),
    )(stay_grads, got_grads)
    result = blocks[0] + jnp.dot(low_mid, down_right, precision=highest)
    input_grad = blocks[1] + lax.dot_general(back_in, up_left, (NT, ((), ())), precision=highest)
    return result, input_grad, up_grad, down_grad, ends[0], up_right_grad, down_left_grad, ends[1]


def solution(mesh):
    return jax.shard_map(
        shards,
        mesh=mesh,
        in_specs=(
            P("dp", "tensor"),
            P("dp", "tensor"),
            P("tensor", None, None),
            P("tensor", None, None),
            P("tensor", None),
            P(None, "tensor"),
            P("tensor", None),
            P(None, "tensor"),
            P("tensor"),
            P("tensor"),
            P("tensor"),
        ),
        out_specs=(
            P("dp", "tensor"),
            P("dp", "tensor"),
            P("tensor", "dp", None),
            P("tensor", "dp", None),
            P(("tensor", "dp"), None),
            P("dp", "tensor"),
            P(("tensor", "dp"), None),
            P("dp", "tensor"),
        ),
        check_vma=False,
    )
```

```python
import jax
import jax.numpy as jnp
from jax import lax
from jax.experimental import pallas as pl
from jax.experimental.pallas import tpu as pltpu
from jax.sharding import PartitionSpec as P

f32 = jnp.float32
highest = lax.Precision.HIGHEST
VMEM = pl.BlockSpec(memory_space=pltpu.VMEM)
HBM = pl.BlockSpec(memory_space=pl.ANY)
SMEM = pl.BlockSpec(memory_space=pltpu.SMEM)
ROOT = 0.7978845608028654
CUBE = 0.044715
BATCH = 4

NN = ((1,), (0,))
NT = ((1,), (1,))
TN = ((0,), (0,))


def split(value):
    high = value.astype(jnp.bfloat16)
    return high, (value - high.astype(f32)).astype(jnp.bfloat16)


def dot3(left, right, dims):
    def one(a, b):
        return lax.dot_general(a, b, (dims, ((), ())), preferred_element_type=f32)

    return one(left[0], right[0]) + (one(left[0], right[1]) + one(left[1], right[0]))


def load(pairs, sems):
    copies = [pltpu.make_async_copy(a, b, sems.at[i]) for i, (a, b) in enumerate(pairs)]
    for copy in copies:
        copy.start()
    return copies


def hidden_kernel(
    model_ref, hidden_ref, live_ref, fields_hbm, up_hbm, down_hbm, low_ref, right_ref, left_ref,
    act_ref, pgrad_ref, part_ref, fields_ref, up_ref, down_ref, sems,
):
    rows = act_ref.shape[1]
    local_blocks = act_ref.shape[0]
    slot_count = up_ref.shape[0]
    copies = load([(fields_hbm, fields_ref), (up_hbm, up_ref), (down_hbm, down_ref)], sems)
    live = live_ref[0]
    low_in = split(low_ref[0:rows])
    back_mid = split(low_ref[rows : 2 * rows])
    for h in range(local_blocks):
        span = slice(h * 128, (h + 1) * 128)
        act_ref[h] = dot3(low_in, split(right_ref[:, span]), NN)
        pgrad_ref[h] = dot3(back_mid, split(left_ref[span]), NT)
    for copy in copies:
        copy.wait()

    @pl.loop(0, slot_count // BATCH)
    def _(step):
        terms = []
        for j in range(BATCH):
            s = step * BATCH + j
            m = model_ref[s]
            alive = jnp.where(s < live, 1.0, 0.0).astype(f32)
            up = dot3(split(fields_ref[m, 0:rows]), split(up_ref[s]), NN)
            back = dot3(split(fields_ref[m, rows : 2 * rows]), split(down_ref[s]), NT)
            terms.append((hidden_ref[s], up * alive, back * alive))
        for h, up, back in terms:
            act_ref[h] += up
            pgrad_ref[h] += back

    low_mid = None
    back_in = None
    for h in range(local_blocks):
        value = act_ref[h]
        square = value * value
        bent = jnp.tanh(ROOT * (value + CUBE * (value * square)))
        half = 0.5 * (1.0 + bent)
        slope = half + 0.5 * value * (1.0 - bent * bent) * (ROOT * (1.0 + 3.0 * CUBE * square))
        hidden = value * half
        pgrad = pgrad_ref[h] * slope
        act_ref[h] = hidden
        pgrad_ref[h] = pgrad
        span = slice(h * 128, (h + 1) * 128)
        mid = dot3(split(hidden), split(left_ref[span]), NN)
        back = dot3(split(pgrad), split(right_ref[:, span]), NT)
        low_mid = mid if low_mid is None else low_mid + mid
        back_in = back if back_in is None else back_in + back
    part_ref[0:rows] = low_mid
    part_ref[rows : 2 * rows] = back_in


def grads_kernel(
    model_ref, hidden_ref, live_ref, group_ref, fields_hbm, after_hbm, act_ref, pgrad_ref, low_ref,
    keep_up_ref, send_up_ref, keep_down_ref, send_down_ref, fields_ref, square_ref, tall_ref, sems,
):
    rows = act_ref.shape[1]
    local_blocks = act_ref.shape[0]
    slot_count = model_ref.shape[0]
    piece = keep_up_ref.shape[3]
    copies = load([(fields_hbm, fields_ref)], sems)
    live = live_ref[0]
    group = group_ref[0]
    low_in = split(low_ref[0:rows])
    back_mid = split(low_ref[rows : 2 * rows])

    def deal(keep_ref, send_ref, near, tile, source, stride, start):
        homes = {0: (keep_ref, 0), near ^ 2: (keep_ref, 1), near: (send_ref, 0), 2: (send_ref, 1)}
        for rel in range(8):
            ref, at = homes[rel >> 1]
            first = pl.multiple_of((group ^ rel) * stride + start, piece)
            ref[at, rel & 1, tile] = source[pl.ds(first, piece)]

    for h in range(local_blocks):
        square_ref[h] = dot3(low_in, split(pgrad_ref[h]), TN)
        deal(keep_up_ref, send_up_ref, 1, slot_count + h, square_ref.at[h], piece, 0)
        tall_ref[h * 128 : (h + 1) * 128] = dot3(split(act_ref[h]), back_mid, TN)
    for i in range(local_blocks):
        deal(keep_down_ref, send_down_ref, 3, slot_count + i, tall_ref, piece * local_blocks, piece * i)
    for copy in copies:
        copy.wait()

    @pl.loop(0, slot_count // BATCH)
    def _(step):
        for j in range(BATCH):
            s = step * BATCH + j
            m = model_ref[s]
            h = hidden_ref[s]
            alive = jnp.where(s < live, 1.0, 0.0).astype(f32)
            square_ref[2 * j] = dot3(split(fields_ref[m, 0:rows]), split(pgrad_ref[h]), TN) * alive
            square_ref[2 * j + 1] = dot3(split(act_ref[h]), split(fields_ref[m, rows : 2 * rows]), TN) * alive
        for j in range(BATCH):
            s = step * BATCH + j
            deal(keep_up_ref, send_up_ref, 1, s, square_ref.at[2 * j], piece, 0)
            deal(keep_down_ref, send_down_ref, 3, s, square_ref.at[2 * j + 1], piece, 0)


def terms_kernel(
    place_ref, hidden_ref, live_ref, up_hbm, down_hbm, act_ref, pgrad_ref,
    keep_ref, send_ref, up_ref, down_ref, sums, sems,
):
    rows = act_ref.shape[1]
    slot_count = up_ref.shape[0]
    copies = load([(up_hbm, up_ref), (down_hbm, down_ref)], sems)
    live = live_ref[0]
    for p in range(2):
        for b in range(16):
            sums[p, b] = jnp.zeros((rows, 128), f32)
    for copy in copies:
        copy.wait()

    @pl.loop(0, slot_count // BATCH)
    def _(step):
        terms = []
        for j in range(BATCH):
            s = step * BATCH + j
            h = hidden_ref[s]
            alive = jnp.where(s < live, 1.0, 0.0).astype(f32)
            out = dot3(split(act_ref[h]), split(down_ref[s]), NN) * alive
            back = dot3(split(pgrad_ref[h]), split(up_ref[s]), NT) * alive
            terms.append((place_ref[s], out, back))
        for b, out, back in terms:
            sums[0, b] += out
            sums[1, b] += back

    keep_ref[...] = sums[:, 0:8]
    send_ref[...] = sums[:, 8:16]


NEAR = (1, 3)


def core_kernel(first_ref, keep_ref, other_ref, after_hbm, hold_ref, send_out_ref, send_back_ref):
    first = first_ref[0]
    for p, send_ref in enumerate((send_out_ref, send_back_ref)):
        near = NEAR[p]
        homes = {0: (hold_ref.at[p], 0), near ^ 2: (hold_ref.at[p], 3), near: (send_ref, 0), 2: (send_ref, 3)}
        for e in range(4):
            ref, at = homes[e]
            ref[at] = keep_ref[p, e] + other_ref[p, e]
            mine = jnp.where(first == (e >> 1), 1.0, 0.0).astype(f32)
            for i in (1, 2):
                b = 2 + 2 * i + (e & 1)
                ref[at + i] = keep_ref[p, b] * mine + other_ref[p, b] * (1.0 - mine)


def near_kernel(hold_ref, got_out_ref, got_back_ref, stay_ref, send_out_ref, send_back_ref):
    for p, (got_ref, send_ref) in enumerate(((got_out_ref, send_out_ref), (got_back_ref, send_back_ref))):
        for f in range(4):
            for pair in range(2):
                total = hold_ref[p, 3 * pair + f] if f < 3 else None
                g = f ^ NEAR[p]
                if g < 3:
                    add = got_ref[3 * pair + g]
                    total = add if total is None else total + add
                if pair:
                    send_ref[f] = total
                else:
                    stay_ref[p, f] = total


def far_kernel(w_ref, stay_ref, got_out_ref, got_back_ref, hold_ref, send_ref):
    w = w_ref[0]
    for flip, ref, at in ((0, hold_ref, 0), (2, hold_ref, 1), (1, send_ref, 0), (3, send_ref, 1)):
        f = w ^ flip
        for p, got_ref in enumerate((got_out_ref, got_back_ref)):
            ref[at, p] = stay_ref[p, f] + got_ref[f ^ (NEAR[p] ^ 2)]


def y_kernel(keep_up_ref, got_up_ref, keep_down_ref, got_down_ref, after_hbm, hold_ref, send_up_ref, send_down_ref):
    hold_ref[0] = keep_up_ref[0] + got_up_ref[0]
    hold_ref[1] = keep_down_ref[0] + got_down_ref[0]
    send_up_ref[...] = keep_up_ref[1] + got_up_ref[1]
    send_down_ref[...] = keep_down_ref[1] + got_down_ref[1]


def ring_kernel(hold_ref, got_up_ref, got_down_ref, after_hbm, stay_ref, send_ref):
    for p, got_ref in enumerate((got_up_ref, got_down_ref)):
        stay_ref[p] = hold_ref[p, 0] + got_ref[0]
        send_ref[p] = hold_ref[p, 1] + got_ref[1]


def last_kernel(stay_ref, got_ref, up_ref, right_ref, down_ref, left_ref):
    slot_count, piece, _ = up_ref.shape
    up_ref[...] = stay_ref[0, 0:slot_count] + got_ref[0, 0:slot_count]
    down_ref[...] = stay_ref[1, 0:slot_count] + got_ref[1, 0:slot_count]
    for h in range(right_ref.shape[1] // 128):
        right_ref[:, h * 128 : (h + 1) * 128] = stay_ref[0, slot_count + h] + got_ref[0, slot_count + h]
        left_ref[h * piece : (h + 1) * piece] = stay_ref[1, slot_count + h] + got_ref[1, slot_count + h]


def pieces_kernel(parts_ref, after_hbm, out_ref):
    total = jnp.sum(parts_ref[...], axis=0)
    for i in range(out_ref.shape[0]):
        out_ref[i] = total


def ends_kernel(inputs_ref, grad_ref, low_ref, after_hbm, out_ref):
    parts, _, piece, _ = out_ref.shape
    rows = inputs_ref.shape[0]
    left = dot3(split(inputs_ref[...]), split(low_ref[rows : 2 * rows]), TN)
    right = dot3(split(low_ref[0:rows]), split(grad_ref[...]), TN)
    out_ref[:, 0] = left.reshape(parts, piece, 128)
    out_ref[:, 1] = right.reshape(parts, piece, 128)


def call(kernel, name, in_specs, outs, scratch=(), mflops=1, kbytes=1000):
    limit = (48 if scratch else 24) * 1024 * 1024
    return pl.pallas_call(
        kernel,
        out_shape=tuple(jax.ShapeDtypeStruct(shape, f32) for shape in outs),
        in_specs=in_specs,
        out_specs=(VMEM,) * len(outs),
        scratch_shapes=list(scratch),
        compiler_params=pltpu.CompilerParams(vmem_limit_bytes=limit),
        cost_estimate=pl.CostEstimate(flops=mflops * 10**6, bytes_accessed=kbytes * 10**3, transcendentals=0),
        name=name,
    )


def xor_shift(value, bits, axis="tensor"):
    return lax.ppermute(value, axis, [(i, i ^ bits) for i in range(lax.axis_size(axis))])


def exchange(value):
    return lax.all_to_all(value, "tensor", 0, 0, tiled=True)


def low_pieces(partial_value):
    size = lax.axis_size("tensor")
    return exchange(partial_value.reshape(size, -1, 128)).sum(axis=0)


def low_whole(pieces):
    size = lax.axis_size("tensor")
    return exchange(jnp.broadcast_to(pieces[None], (size,) + pieces.shape)).reshape(-1, 128)


def shards(
    inputs, out_grad, up_weight, down_weight, up_left, up_right, down_left, down_right,
    model_block, hidden_block, live_slots,
):
    rows = inputs.shape[0]
    slot_count = up_weight.shape[0]
    local_blocks = up_right.shape[1] // 128
    parts = lax.axis_size("dp")
    piece = 128 // parts
    me = lax.axis_index("tensor").astype(jnp.int32)
    core, x, z = me & 1, (me >> 1) & 3, me >> 3
    e = ((model_block >> 1) & 3) ^ x
    zrel = (model_block >> 3) ^ x
    place = jnp.where(zrel == 0, e, 2 + 2 * zrel + (e & 1)) + 8 * ((model_block & 1) ^ core)

    fields = lax.all_gather(jnp.concatenate([inputs, out_grad]), "tensor")
    first_part = jnp.concatenate(
        [
            jnp.dot(inputs, up_left, precision=highest),
            lax.dot_general(out_grad, down_right, (NT, ((), ())), precision=highest),
        ]
    )
    low = low_whole(low_pieces(first_part))
    group = lax.axis_index("dp").astype(jnp.int32)[None]
    local = (local_blocks, rows, 128)
    act, pgrad, low_part = call(
        hidden_kernel,
        "hidden",
        [SMEM] * 3 + [HBM] * 3 + [VMEM] * 3,
        (local, local, (2 * rows, 128)),
        [
            pltpu.VMEM(fields.shape, f32),
            pltpu.VMEM(up_weight.shape, f32),
            pltpu.VMEM(down_weight.shape, f32),
            pltpu.SemaphoreType.DMA((3,)),
        ],
        2000,
        12000,
    )(model_block, hidden_block, live_slots, fields, up_weight, down_weight, low, up_right, down_left)
    keep, send = call(
        terms_kernel,
        "terms",
        [SMEM] * 3 + [HBM] * 2 + [VMEM] * 2,
        ((2, 8, rows, 128),) * 2,
        [
            pltpu.VMEM(up_weight.shape, f32),
            pltpu.VMEM(down_weight.shape, f32),
            pltpu.VMEM((2, 16, rows, 128), f32),
            pltpu.SemaphoreType.DMA((2,)),
        ],
        1500,
        12000,
    )(place, hidden_block, live_slots, up_weight, down_weight, act, pgrad)
    tiles = slot_count + local_blocks
    keep_up, send_up, keep_down, send_down = call(
        grads_kernel,
        "grads",
        [SMEM] * 4 + [HBM] * 2 + [VMEM] * 3,
        ((2, 2, tiles, piece, 128),) * 4,
        [
            pltpu.VMEM(fields.shape, f32),
            pltpu.VMEM((2 * BATCH, 128, 128), f32),
            pltpu.VMEM(down_left.shape, f32),
            pltpu.SemaphoreType.DMA((1,)),
        ],
        1500,
        12000,
    )(model_block, hidden_block, live_slots, group, fields, send, act, pgrad, low)
    got_up = xor_shift(send_up, NEAR[0] << 1, "dp")
    got_down = xor_shift(send_down, NEAR[1] << 1, "dp")
    size = lax.axis_size("tensor")
    low_parts = exchange(low_part.reshape(size, -1, 128))
    other = xor_shift(send, 1)
    hold, send_out, send_back = call(
        core_kernel, "core", [SMEM] + [VMEM] * 2 + [HBM], ((2, 6, rows, 128), (6, rows, 128), (6, rows, 128))
    )(((x // 2) ^ core)[None], keep, other, send_up)
    got_out = xor_shift(send_out, NEAR[0] << 1)
    got_back = xor_shift(send_back, NEAR[1] << 1)
    stay, send_out, send_back = call(
        near_kernel, "near", [VMEM] * 3, ((2, 4, rows, 128), (4, rows, 128), (4, rows, 128))
    )(hold, got_out, got_back)
    half = (2, tiles, piece, 128)
    hold_grads, send_up, send_down = call(
        y_kernel, "ring_y", [VMEM] * 4 + [HBM], ((2,) + half, half, half)
    )(keep_up, got_up, keep_down, got_down, send_out)
    got_up = xor_shift(send_up, NEAR[1] << 1, "dp")
    got_down = xor_shift(send_down, NEAR[0] << 1, "dp")
    got_out = xor_shift(send_out, NEAR[1] << 1)
    got_back = xor_shift(send_back, NEAR[0] << 1)
    pair = (2, 2, rows, 128)
    hold, send = call(far_kernel, "far", [SMEM] + [VMEM] * 3, (pair, pair))((x ^ z)[None], stay, got_out, got_back)
    got = xor_shift(send, 1 << 3)
    send = hold[1] + got[1]
    stay_grads, send_grads = call(ring_kernel, "ring_far", [VMEM] * 3 + [HBM], (half, half))(
        hold_grads, got_up, got_down, send
    )
    got_grads = xor_shift(send_grads, 1, "dp")
    blocks = hold[0] + got[0] + xor_shift(send, 2 << 3)
    (pieces,) = call(pieces_kernel, "pieces", [VMEM, HBM], (low_parts.shape,))(low_parts, send_up)
    lows = exchange(pieces).reshape(-1, 128)
    low_mid, back_in = lows[:rows], lows[rows:]
    (ends,) = call(ends_kernel, "ends", [VMEM] * 3 + [HBM], ((parts, 2, piece, 128),))(
        inputs, out_grad, lows, blocks
    )
    ends = lax.all_to_all(ends, "dp", 0, 0, tiled=True).sum(axis=0)
    up_grad, up_right_grad, down_grad, down_left_grad = call(
        last_kernel,
        "last",
        [VMEM] * 2,
        ((slot_count, piece, 128), (piece, local_blocks * 128), (slot_count, piece, 128), (local_blocks * piece, 128)),
    )(stay_grads, got_grads)
    result = blocks[0] + jnp.dot(low_mid, down_right, precision=highest)
    input_grad = blocks[1] + lax.dot_general(back_in, up_left, (NT, ((), ())), precision=highest)
    return result, input_grad, up_grad, down_grad, ends[0], up_right_grad, down_left_grad, ends[1]


def solution(mesh):
    return jax.shard_map(
        shards,
        mesh=mesh,
        in_specs=(
            P("dp", "tensor"),
            P("dp", "tensor"),
            P("tensor", None, None),
            P("tensor", None, None),
            P("tensor", None),
            P(None, "tensor"),
            P("tensor", None),
            P(None, "tensor"),
            P("tensor"),
            P("tensor"),
            P("tensor"),
        ),
        out_specs=(
            P("dp", "tensor"),
            P("dp", "tensor"),
            P("tensor", "dp", None),
            P("tensor", "dp", None),
            P(("tensor", "dp"), None),
            P("dp", "tensor"),
            P(("tensor", "dp"), None),
            P("dp", "tensor"),
        ),
        check_vma=False,
    )
```

```python
import jax
import jax.numpy as jnp
from jax import lax
from jax.experimental import pallas as pl
from jax.experimental.pallas import tpu as pltpu
from jax.sharding import PartitionSpec as P

f32 = jnp.float32
highest = lax.Precision.HIGHEST
VMEM = pl.BlockSpec(memory_space=pltpu.VMEM)
HBM = pl.BlockSpec(memory_space=pl.ANY)
SMEM = pl.BlockSpec(memory_space=pltpu.SMEM)
ROOT = 0.7978845608028654
CUBE = 0.044715
BATCH = 4

NN = ((1,), (0,))
NT = ((1,), (1,))
TN = ((0,), (0,))


def split(value):
    high = value.astype(jnp.bfloat16)
    return high, (value - high.astype(f32)).astype(jnp.bfloat16)


def dot3(left, right, dims):
    def one(a, b):
        return lax.dot_general(a, b, (dims, ((), ())), preferred_element_type=f32)

    return one(left[0], right[0]) + (one(left[0], right[1]) + one(left[1], right[0]))


def load(pairs, sems):
    copies = [pltpu.make_async_copy(a, b, sems.at[i]) for i, (a, b) in enumerate(pairs)]
    for copy in copies:
        copy.start()
    return copies


def hidden_kernel(
    model_ref, hidden_ref, live_ref, fields_hbm, up_hbm, down_hbm, low_ref, right_ref, left_ref,
    act_ref, pgrad_ref, part_ref, fields_ref, up_ref, down_ref, sems,
):
    rows = act_ref.shape[1]
    local_blocks = act_ref.shape[0]
    slot_count = up_ref.shape[0]
    copies = load([(fields_hbm, fields_ref), (up_hbm, up_ref), (down_hbm, down_ref)], sems)
    live = live_ref[0]
    low_in = split(low_ref[0:rows])
    back_mid = split(low_ref[rows : 2 * rows])
    for h in range(local_blocks):
        span = slice(h * 128, (h + 1) * 128)
        act_ref[h] = dot3(low_in, split(right_ref[:, span]), NN)
        pgrad_ref[h] = dot3(back_mid, split(left_ref[span]), NT)
    for copy in copies:
        copy.wait()

    @pl.loop(0, slot_count // BATCH)
    def _(step):
        terms = []
        for j in range(BATCH):
            s = step * BATCH + j
            m = model_ref[s]
            alive = jnp.where(s < live, 1.0, 0.0).astype(f32)
            up = dot3(split(fields_ref[m, 0:rows]), split(up_ref[s]), NN)
            back = dot3(split(fields_ref[m, rows : 2 * rows]), split(down_ref[s]), NT)
            terms.append((hidden_ref[s], up * alive, back * alive))
        for h, up, back in terms:
            act_ref[h] += up
            pgrad_ref[h] += back

    low_mid = None
    back_in = None
    for h in range(local_blocks):
        value = act_ref[h]
        square = value * value
        bent = jnp.tanh(ROOT * (value + CUBE * (value * square)))
        half = 0.5 * (1.0 + bent)
        slope = half + 0.5 * value * (1.0 - bent * bent) * (ROOT * (1.0 + 3.0 * CUBE * square))
        hidden = value * half
        pgrad = pgrad_ref[h] * slope
        act_ref[h] = hidden
        pgrad_ref[h] = pgrad
        span = slice(h * 128, (h + 1) * 128)
        mid = dot3(split(hidden), split(left_ref[span]), NN)
        back = dot3(split(pgrad), split(right_ref[:, span]), NT)
        low_mid = mid if low_mid is None else low_mid + mid
        back_in = back if back_in is None else back_in + back
    part_ref[0:rows] = low_mid
    part_ref[rows : 2 * rows] = back_in


def grads_kernel(
    model_ref, hidden_ref, live_ref, group_ref, fields_hbm, after_hbm, act_ref, pgrad_ref, low_ref,
    keep_up_ref, send_up_ref, keep_down_ref, send_down_ref, fields_ref, square_ref, tall_ref, sems,
):
    rows = act_ref.shape[1]
    local_blocks = act_ref.shape[0]
    slot_count = model_ref.shape[0]
    piece = keep_up_ref.shape[3]
    copies = load([(fields_hbm, fields_ref)], sems)
    live = live_ref[0]
    group = group_ref[0]
    low_in = split(low_ref[0:rows])
    back_mid = split(low_ref[rows : 2 * rows])

    def deal(keep_ref, send_ref, near, tile, source, stride, start):
        homes = {0: (keep_ref, 0), near ^ 2: (keep_ref, 1), near: (send_ref, 0), 2: (send_ref, 1)}
        for rel in range(8):
            ref, at = homes[rel >> 1]
            first = pl.multiple_of((group ^ rel) * stride + start, piece)
            ref[at, rel & 1, tile] = source[pl.ds(first, piece)]

    for h in range(local_blocks):
        square_ref[h] = dot3(low_in, split(pgrad_ref[h]), TN)
        deal(keep_up_ref, send_up_ref, 1, slot_count + h, square_ref.at[h], piece, 0)
        tall_ref[h * 128 : (h + 1) * 128] = dot3(split(act_ref[h]), back_mid, TN)
    for i in range(local_blocks):
        deal(keep_down_ref, send_down_ref, 3, slot_count + i, tall_ref, piece * local_blocks, piece * i)
    for copy in copies:
        copy.wait()

    @pl.loop(0, slot_count // BATCH)
    def _(step):
        for j in range(BATCH):
            s = step * BATCH + j
            m = model_ref[s]
            h = hidden_ref[s]
            alive = jnp.where(s < live, 1.0, 0.0).astype(f32)
            square_ref[2 * j] = dot3(split(fields_ref[m, 0:rows]), split(pgrad_ref[h]), TN) * alive
            square_ref[2 * j + 1] = dot3(split(act_ref[h]), split(fields_ref[m, rows : 2 * rows]), TN) * alive
        for j in range(BATCH):
            s = step * BATCH + j
            deal(keep_up_ref, send_up_ref, 1, s, square_ref.at[2 * j], piece, 0)
            deal(keep_down_ref, send_down_ref, 3, s, square_ref.at[2 * j + 1], piece, 0)


def terms_kernel(
    place_ref, hidden_ref, live_ref, up_hbm, down_hbm, act_ref, pgrad_ref,
    keep_ref, send_ref, up_ref, down_ref, sums, sems,
):
    rows = act_ref.shape[1]
    slot_count = up_ref.shape[0]
    copies = load([(up_hbm, up_ref), (down_hbm, down_ref)], sems)
    live = live_ref[0]
    for p in range(2):
        for b in range(16):
            sums[p, b] = jnp.zeros((rows, 128), f32)
    for copy in copies:
        copy.wait()

    @pl.loop(0, slot_count // BATCH)
    def _(step):
        terms = []
        for j in range(BATCH):
            s = step * BATCH + j
            h = hidden_ref[s]
            alive = jnp.where(s < live, 1.0, 0.0).astype(f32)
            out = dot3(split(act_ref[h]), split(down_ref[s]), NN) * alive
            back = dot3(split(pgrad_ref[h]), split(up_ref[s]), NT) * alive
            terms.append((place_ref[s], out, back))
        for b, out, back in terms:
            sums[0, b] += out
            sums[1, b] += back

    keep_ref[...] = sums[:, 0:8]
    send_ref[...] = sums[:, 8:16]


NEAR = (1, 3)


def core_kernel(first_ref, keep_ref, other_ref, after_hbm, hold_ref, send_out_ref, send_back_ref):
    first = first_ref[0]
    for p, send_ref in enumerate((send_out_ref, send_back_ref)):
        near = NEAR[p]
        homes = {0: (hold_ref.at[p], 0), near ^ 2: (hold_ref.at[p], 3), near: (send_ref, 0), 2: (send_ref, 3)}
        for e in range(4):
            ref, at = homes[e]
            ref[at] = keep_ref[p, e] + other_ref[p, e]
            mine = jnp.where(first == (e >> 1), 1.0, 0.0).astype(f32)
            for i in (1, 2):
                b = 2 + 2 * i + (e & 1)
                ref[at + i] = keep_ref[p, b] * mine + other_ref[p, b] * (1.0 - mine)


def near_kernel(hold_ref, got_out_ref, got_back_ref, stay_ref, send_out_ref, send_back_ref):
    for p, (got_ref, send_ref) in enumerate(((got_out_ref, send_out_ref), (got_back_ref, send_back_ref))):
        for f in range(4):
            for pair in range(2):
                total = hold_ref[p, 3 * pair + f] if f < 3 else None
                g = f ^ NEAR[p]
                if g < 3:
                    add = got_ref[3 * pair + g]
                    total = add if total is None else total + add
                if pair:
                    send_ref[f] = total
                else:
                    stay_ref[p, f] = total


def far_kernel(w_ref, stay_ref, got_out_ref, got_back_ref, hold_ref, send_ref):
    w = w_ref[0]
    for flip, ref, at in ((0, hold_ref, 0), (2, hold_ref, 1), (1, send_ref, 0), (3, send_ref, 1)):
        f = w ^ flip
        for p, got_ref in enumerate((got_out_ref, got_back_ref)):
            ref[at, p] = stay_ref[p, f] + got_ref[f ^ (NEAR[p] ^ 2)]


def y_kernel(keep_up_ref, got_up_ref, keep_down_ref, got_down_ref, after_hbm, hold_ref, send_up_ref, send_down_ref):
    hold_ref[0] = keep_up_ref[0] + got_up_ref[0]
    hold_ref[1] = keep_down_ref[0] + got_down_ref[0]
    send_up_ref[...] = keep_up_ref[1] + got_up_ref[1]
    send_down_ref[...] = keep_down_ref[1] + got_down_ref[1]


def ring_kernel(hold_ref, got_up_ref, got_down_ref, after_hbm, stay_ref, send_ref):
    for p, got_ref in enumerate((got_up_ref, got_down_ref)):
        stay_ref[p] = hold_ref[p, 0] + got_ref[0]
        send_ref[p] = hold_ref[p, 1] + got_ref[1]


def last_kernel(stay_ref, got_ref, up_ref, right_ref, down_ref, left_ref):
    slot_count, piece, _ = up_ref.shape
    up_ref[...] = stay_ref[0, 0:slot_count] + got_ref[0, 0:slot_count]
    down_ref[...] = stay_ref[1, 0:slot_count] + got_ref[1, 0:slot_count]
    for h in range(right_ref.shape[1] // 128):
        right_ref[:, h * 128 : (h + 1) * 128] = stay_ref[0, slot_count + h] + got_ref[0, slot_count + h]
        left_ref[h * piece : (h + 1) * piece] = stay_ref[1, slot_count + h] + got_ref[1, slot_count + h]


def pieces_kernel(parts_ref, after_hbm, out_ref):
    total = jnp.sum(parts_ref[...], axis=0)
    for i in range(out_ref.shape[0]):
        out_ref[i] = total


def ends_kernel(inputs_ref, grad_ref, low_ref, after_hbm, out_ref):
    parts, _, piece, _ = out_ref.shape
    rows = inputs_ref.shape[0]
    left = dot3(split(inputs_ref[...]), split(low_ref[rows : 2 * rows]), TN)
    right = dot3(split(low_ref[0:rows]), split(grad_ref[...]), TN)
    out_ref[:, 0] = left.reshape(parts, piece, 128)
    out_ref[:, 1] = right.reshape(parts, piece, 128)


def call(kernel, name, in_specs, outs, scratch=(), mflops=1, kbytes=1000):
    limit = (48 if scratch else 24) * 1024 * 1024
    return pl.pallas_call(
        kernel,
        out_shape=tuple(jax.ShapeDtypeStruct(shape, f32) for shape in outs),
        in_specs=in_specs,
        out_specs=(VMEM,) * len(outs),
        scratch_shapes=list(scratch),
        compiler_params=pltpu.CompilerParams(vmem_limit_bytes=limit),
        cost_estimate=pl.CostEstimate(flops=mflops * 10**6, bytes_accessed=kbytes * 10**3, transcendentals=0),
        name=name,
    )


def xor_shift(value, bits, axis="tensor"):
    return lax.ppermute(value, axis, [(i, i ^ bits) for i in range(lax.axis_size(axis))])


def exchange(value):
    return lax.all_to_all(value, "tensor", 0, 0, tiled=True)


def low_pieces(partial_value):
    size = lax.axis_size("tensor")
    return exchange(partial_value.reshape(size, -1, 128)).sum(axis=0)


def low_whole(pieces):
    size = lax.axis_size("tensor")
    return exchange(jnp.broadcast_to(pieces[None], (size,) + pieces.shape)).reshape(-1, 128)


def shards(
    inputs, out_grad, up_weight, down_weight, up_left, up_right, down_left, down_right,
    model_block, hidden_block, live_slots,
):
    rows = inputs.shape[0]
    slot_count = up_weight.shape[0]
    local_blocks = up_right.shape[1] // 128
    parts = lax.axis_size("dp")
    piece = 128 // parts
    me = lax.axis_index("tensor").astype(jnp.int32)
    core, x, z = me & 1, (me >> 1) & 3, me >> 3
    e = ((model_block >> 1) & 3) ^ x
    zrel = (model_block >> 3) ^ x
    place = jnp.where(zrel == 0, e, 2 + 2 * zrel + (e & 1)) + 8 * ((model_block & 1) ^ core)

    fields = lax.all_gather(jnp.concatenate([inputs, out_grad]), "tensor")
    first_part = jnp.concatenate(
        [
            jnp.dot(inputs, up_left, precision=highest),
            lax.dot_general(out_grad, down_right, (NT, ((), ())), precision=highest),
        ]
    )
    low = low_whole(low_pieces(first_part))
    group = lax.axis_index("dp").astype(jnp.int32)[None]
    local = (local_blocks, rows, 128)
    act, pgrad, low_part = call(
        hidden_kernel,
        "hidden",
        [SMEM] * 3 + [HBM] * 3 + [VMEM] * 3,
        (local, local, (2 * rows, 128)),
        [
            pltpu.VMEM(fields.shape, f32),
            pltpu.VMEM(up_weight.shape, f32),
            pltpu.VMEM(down_weight.shape, f32),
            pltpu.SemaphoreType.DMA((3,)),
        ],
        2000,
        12000,
    )(model_block, hidden_block, live_slots, fields, up_weight, down_weight, low, up_right, down_left)
    keep, send = call(
        terms_kernel,
        "terms",
        [SMEM] * 3 + [HBM] * 2 + [VMEM] * 2,
        ((2, 8, rows, 128),) * 2,
        [
            pltpu.VMEM(up_weight.shape, f32),
            pltpu.VMEM(down_weight.shape, f32),
            pltpu.VMEM((2, 16, rows, 128), f32),
            pltpu.SemaphoreType.DMA((2,)),
        ],
        1500,
        12000,
    )(place, hidden_block, live_slots, up_weight, down_weight, act, pgrad)
    tiles = slot_count + local_blocks
    keep_up, send_up, keep_down, send_down = call(
        grads_kernel,
        "grads",
        [SMEM] * 4 + [HBM] * 2 + [VMEM] * 3,
        ((2, 2, tiles, piece, 128),) * 4,
        [
            pltpu.VMEM(fields.shape, f32),
            pltpu.VMEM((2 * BATCH, 128, 128), f32),
            pltpu.VMEM(down_left.shape, f32),
            pltpu.SemaphoreType.DMA((1,)),
        ],
        1500,
        12000,
    )(model_block, hidden_block, live_slots, group, fields, send, act, pgrad, low)
    got_up = xor_shift(send_up, NEAR[0] << 1, "dp")
    got_down = xor_shift(send_down, NEAR[1] << 1, "dp")
    size = lax.axis_size("tensor")
    low_parts = exchange(low_part.reshape(size, -1, 128))
    other = xor_shift(send, 1)
    hold, send_out, send_back = call(
        core_kernel, "core", [SMEM] + [VMEM] * 2 + [HBM], ((2, 6, rows, 128), (6, rows, 128), (6, rows, 128))
    )(((x // 2) ^ core)[None], keep, other, send_up)
    got_out = xor_shift(send_out, NEAR[0] << 1)
    got_back = xor_shift(send_back, NEAR[1] << 1)
    stay, send_out, send_back = call(
        near_kernel, "near", [VMEM] * 3, ((2, 4, rows, 128), (4, rows, 128), (4, rows, 128))
    )(hold, got_out, got_back)
    half = (2, tiles, piece, 128)
    hold_grads, send_up, send_down = call(
        y_kernel, "ring_y", [VMEM] * 4 + [HBM], ((2,) + half, half, half)
    )(keep_up, got_up, keep_down, got_down, send_out)
    got_up = xor_shift(send_up, NEAR[1] << 1, "dp")
    got_down = xor_shift(send_down, NEAR[0] << 1, "dp")
    got_out = xor_shift(send_out, NEAR[1] << 1)
    got_back = xor_shift(send_back, NEAR[0] << 1)
    pair = (2, 2, rows, 128)
    hold, send = call(far_kernel, "far", [SMEM] + [VMEM] * 3, (pair, pair))((x ^ z)[None], stay, got_out, got_back)
    got = xor_shift(send, 1 << 3)
    send = hold[1] + got[1]
    stay_grads, send_grads = call(ring_kernel, "ring_far", [VMEM] * 3 + [HBM], (half, half))(
        hold_grads, got_up, got_down, send
    )
    got_grads = xor_shift(send_grads, 1, "dp")
    blocks = hold[0] + got[0] + xor_shift(send, 2 << 3)
    (pieces,) = call(pieces_kernel, "pieces", [VMEM, HBM], (low_parts.shape,))(low_parts, send)
    lows = exchange(pieces).reshape(-1, 128)
    low_mid, back_in = lows[:rows], lows[rows:]
    (ends,) = call(ends_kernel, "ends", [VMEM] * 3 + [HBM], ((parts, 2, piece, 128),))(
        inputs, out_grad, lows, blocks
    )
    ends = lax.all_to_all(ends, "dp", 0, 0, tiled=True).sum(axis=0)
    up_grad, up_right_grad, down_grad, down_left_grad = call(
        last_kernel,
        "last",
        [VMEM] * 2,
        ((slot_count, piece, 128), (piece, local_blocks * 128), (slot_count, piece, 128), (local_blocks * piece, 128)),
    )(stay_grads, got_grads)
    result = blocks[0] + jnp.dot(low_mid, down_right, precision=highest)
    input_grad = blocks[1] + lax.dot_general(back_in, up_left, (NT, ((), ())), precision=highest)
    return result, input_grad, up_grad, down_grad, ends[0], up_right_grad, down_left_grad, ends[1]


def solution(mesh):
    return jax.shard_map(
        shards,
        mesh=mesh,
        in_specs=(
            P("dp", "tensor"),
            P("dp", "tensor"),
            P("tensor", None, None),
            P("tensor", None, None),
            P("tensor", None),
            P(None, "tensor"),
            P("tensor", None),
            P(None, "tensor"),
            P("tensor"),
            P("tensor"),
            P("tensor"),
        ),
        out_specs=(
            P("dp", "tensor"),
            P("dp", "tensor"),
            P("tensor", "dp", None),
            P("tensor", "dp", None),
            P(("tensor", "dp"), None),
            P("dp", "tensor"),
            P(("tensor", "dp"), None),
            P("dp", "tensor"),
        ),
        check_vma=False,
    )
```

```python
import jax
import jax.numpy as jnp
from jax import lax
from jax.experimental import pallas as pl
from jax.experimental.pallas import tpu as pltpu
from jax.sharding import PartitionSpec as P

f32 = jnp.float32
highest = lax.Precision.HIGHEST
VMEM = pl.BlockSpec(memory_space=pltpu.VMEM)
HBM = pl.BlockSpec(memory_space=pl.ANY)
SMEM = pl.BlockSpec(memory_space=pltpu.SMEM)
ROOT = 0.7978845608028654
CUBE = 0.044715
BATCH = 4

NN = ((1,), (0,))
NT = ((1,), (1,))
TN = ((0,), (0,))


def split(value):
    high = value.astype(jnp.bfloat16)
    return high, (value - high.astype(f32)).astype(jnp.bfloat16)


def dot3(left, right, dims):
    def one(a, b):
        return lax.dot_general(a, b, (dims, ((), ())), preferred_element_type=f32)

    return one(left[0], right[0]) + (one(left[0], right[1]) + one(left[1], right[0]))


def load(pairs, sems):
    copies = [pltpu.make_async_copy(a, b, sems.at[i]) for i, (a, b) in enumerate(pairs)]
    for copy in copies:
        copy.start()
    return copies


def hidden_kernel(
    model_ref, hidden_ref, live_ref, fields_hbm, up_hbm, down_hbm, low_ref, right_ref, left_ref,
    act_ref, pgrad_ref, part_ref, fields_ref, up_ref, down_ref, sems,
):
    rows = act_ref.shape[1]
    local_blocks = act_ref.shape[0]
    slot_count = up_ref.shape[0]
    copies = load([(fields_hbm, fields_ref), (up_hbm, up_ref), (down_hbm, down_ref)], sems)
    live = live_ref[0]
    low_in = split(low_ref[0:rows])
    back_mid = split(low_ref[rows : 2 * rows])
    for h in range(local_blocks):
        span = slice(h * 128, (h + 1) * 128)
        act_ref[h] = dot3(low_in, split(right_ref[:, span]), NN)
        pgrad_ref[h] = dot3(back_mid, split(left_ref[span]), NT)
    for copy in copies:
        copy.wait()

    @pl.loop(0, slot_count // BATCH)
    def _(step):
        terms = []
        for j in range(BATCH):
            s = step * BATCH + j
            m = model_ref[s]
            alive = jnp.where(s < live, 1.0, 0.0).astype(f32)
            up = dot3(split(fields_ref[m, 0:rows]), split(up_ref[s]), NN)
            back = dot3(split(fields_ref[m, rows : 2 * rows]), split(down_ref[s]), NT)
            terms.append((hidden_ref[s], up * alive, back * alive))
        for h, up, back in terms:
            act_ref[h] += up
            pgrad_ref[h] += back

    low_mid = None
    back_in = None
    for h in range(local_blocks):
        value = act_ref[h]
        square = value * value
        bent = jnp.tanh(ROOT * (value + CUBE * (value * square)))
        half = 0.5 * (1.0 + bent)
        slope = half + 0.5 * value * (1.0 - bent * bent) * (ROOT * (1.0 + 3.0 * CUBE * square))
        hidden = value * half
        pgrad = pgrad_ref[h] * slope
        act_ref[h] = hidden
        pgrad_ref[h] = pgrad
        span = slice(h * 128, (h + 1) * 128)
        mid = dot3(split(hidden), split(left_ref[span]), NN)
        back = dot3(split(pgrad), split(right_ref[:, span]), NT)
        low_mid = mid if low_mid is None else low_mid + mid
        back_in = back if back_in is None else back_in + back
    part_ref[0:rows] = low_mid
    part_ref[rows : 2 * rows] = back_in


def grads_kernel(
    model_ref, hidden_ref, live_ref, group_ref, fields_hbm, after_hbm, act_ref, pgrad_ref, low_ref,
    keep_up_ref, send_up_ref, keep_down_ref, send_down_ref, fields_ref, square_ref, tall_ref, sems,
):
    rows = act_ref.shape[1]
    local_blocks = act_ref.shape[0]
    slot_count = model_ref.shape[0]
    piece = keep_up_ref.shape[3]
    copies = load([(fields_hbm, fields_ref)], sems)
    live = live_ref[0]
    group = group_ref[0]
    low_in = split(low_ref[0:rows])
    back_mid = split(low_ref[rows : 2 * rows])

    def deal(keep_ref, send_ref, near, tile, source, stride, start):
        homes = {0: (keep_ref, 0), near ^ 2: (keep_ref, 1), near: (send_ref, 0), 2: (send_ref, 1)}
        for rel in range(8):
            ref, at = homes[rel >> 1]
            first = pl.multiple_of((group ^ rel) * stride + start, piece)
            ref[at, rel & 1, tile] = source[pl.ds(first, piece)]

    for h in range(local_blocks):
        square_ref[h] = dot3(low_in, split(pgrad_ref[h]), TN)
        deal(keep_up_ref, send_up_ref, 1, slot_count + h, square_ref.at[h], piece, 0)
        tall_ref[h * 128 : (h + 1) * 128] = dot3(split(act_ref[h]), back_mid, TN)
    for i in range(local_blocks):
        deal(keep_down_ref, send_down_ref, 3, slot_count + i, tall_ref, piece * local_blocks, piece * i)
    for copy in copies:
        copy.wait()

    @pl.loop(0, slot_count // BATCH)
    def _(step):
        for j in range(BATCH):
            s = step * BATCH + j
            m = model_ref[s]
            h = hidden_ref[s]
            alive = jnp.where(s < live, 1.0, 0.0).astype(f32)
            square_ref[2 * j] = dot3(split(fields_ref[m, 0:rows]), split(pgrad_ref[h]), TN) * alive
            square_ref[2 * j + 1] = dot3(split(act_ref[h]), split(fields_ref[m, rows : 2 * rows]), TN) * alive
        for j in range(BATCH):
            s = step * BATCH + j
            deal(keep_up_ref, send_up_ref, 1, s, square_ref.at[2 * j], piece, 0)
            deal(keep_down_ref, send_down_ref, 3, s, square_ref.at[2 * j + 1], piece, 0)


def terms_kernel(
    place_ref, hidden_ref, live_ref, up_hbm, down_hbm, act_ref, pgrad_ref,
    keep_ref, send_ref, up_ref, down_ref, sums, sems,
):
    rows = act_ref.shape[1]
    slot_count = up_ref.shape[0]
    copies = load([(up_hbm, up_ref), (down_hbm, down_ref)], sems)
    live = live_ref[0]
    for p in range(2):
        for b in range(16):
            sums[p, b] = jnp.zeros((rows, 128), f32)
    for copy in copies:
        copy.wait()

    @pl.loop(0, slot_count // BATCH)
    def _(step):
        terms = []
        for j in range(BATCH):
            s = step * BATCH + j
            h = hidden_ref[s]
            alive = jnp.where(s < live, 1.0, 0.0).astype(f32)
            out = dot3(split(act_ref[h]), split(down_ref[s]), NN) * alive
            back = dot3(split(pgrad_ref[h]), split(up_ref[s]), NT) * alive
            terms.append((place_ref[s], out, back))
        for b, out, back in terms:
            sums[0, b] += out
            sums[1, b] += back

    keep_ref[...] = sums[:, 0:8]
    send_ref[...] = sums[:, 8:16]


NEAR = (1, 3)


def core_kernel(first_ref, keep_ref, other_ref, after_hbm, hold_ref, send_out_ref, send_back_ref):
    first = first_ref[0]
    for p, send_ref in enumerate((send_out_ref, send_back_ref)):
        near = NEAR[p]
        homes = {0: (hold_ref.at[p], 0), near ^ 2: (hold_ref.at[p], 3), near: (send_ref, 0), 2: (send_ref, 3)}
        for e in range(4):
            ref, at = homes[e]
            ref[at] = keep_ref[p, e] + other_ref[p, e]
            mine = jnp.where(first == (e >> 1), 1.0, 0.0).astype(f32)
            for i in (1, 2):
                b = 2 + 2 * i + (e & 1)
                ref[at + i] = keep_ref[p, b] * mine + other_ref[p, b] * (1.0 - mine)


def near_kernel(hold_ref, got_out_ref, got_back_ref, stay_ref, send_out_ref, send_back_ref):
    for p, (got_ref, send_ref) in enumerate(((got_out_ref, send_out_ref), (got_back_ref, send_back_ref))):
        for f in range(4):
            for pair in range(2):
                total = hold_ref[p, 3 * pair + f] if f < 3 else None
                g = f ^ NEAR[p]
                if g < 3:
                    add = got_ref[3 * pair + g]
                    total = add if total is None else total + add
                if pair:
                    send_ref[f] = total
                else:
                    stay_ref[p, f] = total


def far_kernel(w_ref, stay_ref, got_out_ref, got_back_ref, hold_ref, send_ref):
    w = w_ref[0]
    for flip, ref, at in ((0, hold_ref, 0), (2, hold_ref, 1), (1, send_ref, 0), (3, send_ref, 1)):
        f = w ^ flip
        for p, got_ref in enumerate((got_out_ref, got_back_ref)):
            ref[at, p] = stay_ref[p, f] + got_ref[f ^ (NEAR[p] ^ 2)]


def y_kernel(keep_up_ref, got_up_ref, keep_down_ref, got_down_ref, after_hbm, hold_ref, send_up_ref, send_down_ref):
    hold_ref[0] = keep_up_ref[0] + got_up_ref[0]
    hold_ref[1] = keep_down_ref[0] + got_down_ref[0]
    send_up_ref[...] = keep_up_ref[1] + got_up_ref[1]
    send_down_ref[...] = keep_down_ref[1] + got_down_ref[1]


def ring_kernel(hold_ref, got_up_ref, got_down_ref, after_hbm, stay_ref, send_ref):
    for p, got_ref in enumerate((got_up_ref, got_down_ref)):
        stay_ref[p] = hold_ref[p, 0] + got_ref[0]
        send_ref[p] = hold_ref[p, 1] + got_ref[1]


def last_kernel(stay_ref, got_ref, up_ref, right_ref, down_ref, left_ref):
    slot_count, piece, _ = up_ref.shape
    up_ref[...] = stay_ref[0, 0:slot_count] + got_ref[0, 0:slot_count]
    down_ref[...] = stay_ref[1, 0:slot_count] + got_ref[1, 0:slot_count]
    for h in range(right_ref.shape[1] // 128):
        right_ref[:, h * 128 : (h + 1) * 128] = stay_ref[0, slot_count + h] + got_ref[0, slot_count + h]
        left_ref[h * piece : (h + 1) * piece] = stay_ref[1, slot_count + h] + got_ref[1, slot_count + h]


def pieces_kernel(parts_ref, after_hbm, out_ref):
    total = jnp.sum(parts_ref[...], axis=0)
    for i in range(out_ref.shape[0]):
        out_ref[i] = total


def ends_kernel(inputs_ref, grad_ref, low_ref, after_hbm, out_ref):
    parts, _, piece, _ = out_ref.shape
    rows = inputs_ref.shape[0]
    left = dot3(split(inputs_ref[...]), split(low_ref[rows : 2 * rows]), TN)
    right = dot3(split(low_ref[0:rows]), split(grad_ref[...]), TN)
    out_ref[:, 0] = left.reshape(parts, piece, 128)
    out_ref[:, 1] = right.reshape(parts, piece, 128)


def call(kernel, name, in_specs, outs, scratch=(), mflops=1, kbytes=1000):
    limit = (48 if scratch else 24) * 1024 * 1024
    return pl.pallas_call(
        kernel,
        out_shape=tuple(jax.ShapeDtypeStruct(shape, f32) for shape in outs),
        in_specs=in_specs,
        out_specs=(VMEM,) * len(outs),
        scratch_shapes=list(scratch),
        compiler_params=pltpu.CompilerParams(vmem_limit_bytes=limit),
        cost_estimate=pl.CostEstimate(flops=mflops * 10**6, bytes_accessed=kbytes * 10**3, transcendentals=0),
        name=name,
    )


def xor_shift(value, bits, axis="tensor"):
    return lax.ppermute(value, axis, [(i, i ^ bits) for i in range(lax.axis_size(axis))])


def exchange(value):
    return lax.all_to_all(value, "tensor", 0, 0, tiled=True)


def low_pieces(partial_value):
    size = lax.axis_size("tensor")
    return exchange(partial_value.reshape(size, -1, 128)).sum(axis=0)


def low_whole(pieces):
    size = lax.axis_size("tensor")
    return exchange(jnp.broadcast_to(pieces[None], (size,) + pieces.shape)).reshape(-1, 128)


def shards(
    inputs, out_grad, up_weight, down_weight, up_left, up_right, down_left, down_right,
    model_block, hidden_block, live_slots,
):
    rows = inputs.shape[0]
    slot_count = up_weight.shape[0]
    local_blocks = up_right.shape[1] // 128
    parts = lax.axis_size("dp")
    piece = 128 // parts
    me = lax.axis_index("tensor").astype(jnp.int32)
    core, x, z = me & 1, (me >> 1) & 3, me >> 3
    e = ((model_block >> 1) & 3) ^ x
    zrel = (model_block >> 3) ^ x
    place = jnp.where(zrel == 0, e, 2 + 2 * zrel + (e & 1)) + 8 * ((model_block & 1) ^ core)

    fields = lax.all_gather(jnp.concatenate([inputs, out_grad]), "tensor")
    first_part = jnp.concatenate(
        [
            jnp.dot(inputs, up_left, precision=highest),
            lax.dot_general(out_grad, down_right, (NT, ((), ())), precision=highest),
        ]
    )
    low = low_whole(low_pieces(first_part))
    group = lax.axis_index("dp").astype(jnp.int32)[None]
    local = (local_blocks, rows, 128)
    act, pgrad, low_part = call(
        hidden_kernel,
        "hidden",
        [SMEM] * 3 + [HBM] * 3 + [VMEM] * 3,
        (local, local, (2 * rows, 128)),
        [
            pltpu.VMEM(fields.shape, f32),
            pltpu.VMEM(up_weight.shape, f32),
            pltpu.VMEM(down_weight.shape, f32),
            pltpu.SemaphoreType.DMA((3,)),
        ],
        2000,
        12000,
    )(model_block, hidden_block, live_slots, fields, up_weight, down_weight, low, up_right, down_left)
    keep, send = call(
        terms_kernel,
        "terms",
        [SMEM] * 3 + [HBM] * 2 + [VMEM] * 2,
        ((2, 8, rows, 128),) * 2,
        [
            pltpu.VMEM(up_weight.shape, f32),
            pltpu.VMEM(down_weight.shape, f32),
            pltpu.VMEM((2, 16, rows, 128), f32),
            pltpu.SemaphoreType.DMA((2,)),
        ],
        1500,
        12000,
    )(place, hidden_block, live_slots, up_weight, down_weight, act, pgrad)
    tiles = slot_count + local_blocks
    keep_up, send_up, keep_down, send_down = call(
        grads_kernel,
        "grads",
        [SMEM] * 4 + [HBM] * 2 + [VMEM] * 3,
        ((2, 2, tiles, piece, 128),) * 4,
        [
            pltpu.VMEM(fields.shape, f32),
            pltpu.VMEM((2 * BATCH, 128, 128), f32),
            pltpu.VMEM(down_left.shape, f32),
            pltpu.SemaphoreType.DMA((1,)),
        ],
        1500,
        12000,
    )(model_block, hidden_block, live_slots, group, fields, send, act, pgrad, low)
    got_up = xor_shift(send_up, NEAR[0] << 1, "dp")
    got_down = xor_shift(send_down, NEAR[1] << 1, "dp")
    size = lax.axis_size("tensor")
    low_parts = exchange(low_part.reshape(size, -1, 128))
    other = xor_shift(send, 1)
    hold, send_out, send_back = call(
        core_kernel, "core", [SMEM] + [VMEM] * 2 + [HBM], ((2, 6, rows, 128), (6, rows, 128), (6, rows, 128))
    )(((x // 2) ^ core)[None], keep, other, send_up)
    got_out = xor_shift(send_out, NEAR[0] << 1)
    got_back = xor_shift(send_back, NEAR[1] << 1)
    stay, send_out, send_back = call(
        near_kernel, "near", [VMEM] * 3, ((2, 4, rows, 128), (4, rows, 128), (4, rows, 128))
    )(hold, got_out, got_back)
    half = (2, tiles, piece, 128)
    hold_grads, send_up, send_down = call(
        y_kernel, "ring_y", [VMEM] * 4 + [HBM], ((2,) + half, half, half)
    )(keep_up, got_up, keep_down, got_down, send_out)
    got_up = xor_shift(send_up, NEAR[1] << 1, "dp")
    got_down = xor_shift(send_down, NEAR[0] << 1, "dp")
    got_out = xor_shift(send_out, NEAR[1] << 1)
    got_back = xor_shift(send_back, NEAR[0] << 1)
    pair = (2, 2, rows, 128)
    hold, send = call(far_kernel, "far", [SMEM] + [VMEM] * 3, (pair, pair))((x ^ z)[None], stay, got_out, got_back)
    (pieces,) = call(pieces_kernel, "pieces", [VMEM, HBM], (low_parts.shape,))(low_parts, send)
    got = xor_shift(send, 1 << 3)
    send = hold[1] + got[1]
    stay_grads, send_grads = call(ring_kernel, "ring_far", [VMEM] * 3 + [HBM], (half, half))(
        hold_grads, got_up, got_down, send
    )
    got_grads = xor_shift(send_grads, 1, "dp")
    blocks = hold[0] + got[0] + xor_shift(send, 2 << 3)
    lows = exchange(pieces).reshape(-1, 128)
    low_mid, back_in = lows[:rows], lows[rows:]
    (ends,) = call(ends_kernel, "ends", [VMEM] * 3 + [HBM], ((parts, 2, piece, 128),))(
        inputs, out_grad, lows, send
    )
    ends = lax.all_to_all(ends, "dp", 0, 0, tiled=True).sum(axis=0)
    up_grad, up_right_grad, down_grad, down_left_grad = call(
        last_kernel,
        "last",
        [VMEM] * 2,
        ((slot_count, piece, 128), (piece, local_blocks * 128), (slot_count, piece, 128), (local_blocks * piece, 128)),
    )(stay_grads, got_grads)
    result = blocks[0] + jnp.dot(low_mid, down_right, precision=highest)
    input_grad = blocks[1] + lax.dot_general(back_in, up_left, (NT, ((), ())), precision=highest)
    return result, input_grad, up_grad, down_grad, ends[0], up_right_grad, down_left_grad, ends[1]


def solution(mesh):
    return jax.shard_map(
        shards,
        mesh=mesh,
        in_specs=(
            P("dp", "tensor"),
            P("dp", "tensor"),
            P("tensor", None, None),
            P("tensor", None, None),
            P("tensor", None),
            P(None, "tensor"),
            P("tensor", None),
            P(None, "tensor"),
            P("tensor"),
            P("tensor"),
            P("tensor"),
        ),
        out_specs=(
            P("dp", "tensor"),
            P("dp", "tensor"),
            P("tensor", "dp", None),
            P("tensor", "dp", None),
            P(("tensor", "dp"), None),
            P("dp", "tensor"),
            P(("tensor", "dp"), None),
            P("dp", "tensor"),
        ),
        check_vma=False,
    )
```
